128 devices in a mesh: gx: 8 (over x_hi, z), gy: 16 (over y, x_lo, core).
Axes of the slice: x: 4 (x_hi: 2, x_lo: 2; x = x_hi * 2 + x_lo), y: 4, z: 4, core: 2. Of those that a mesh axis runs over, the one named last changes fastest.
Arguments:
- weights: bfloat16 [2097152, 128], P(('gx', 'gy')), may hold values from -6 to 6
- travel: float32 [2097152, 64], P(('gx', 'gy')), may hold values from -3.140625 to 3.140625
- interp_real: bfloat16 [8, 2, 2, 64, 64], replicated, may hold values from -0.375 to 0.375
- interp_imag: bfloat16 [8, 2, 2, 64, 64], replicated, may hold values from -0.375 to 0.375
- eval_real: bfloat16 [64, 64], replicated, may hold values from -0.5 to 0.5
- eval_imag: bfloat16 [64, 64], replicated, may hold values from -0.5 to 0.5
Outputs:
- image: bfloat16 [2097152, 128], P(('gx', 'gy'))
The draws below stay inside these ranges and needn't reach their ends.
All inputs are finite; a program needn't handle non-finite values.
Results may differ from the reference program's by a relative error of at most 0.013.
Values may be sent and summed in bfloat16 or wider, within the bound.
A program may use at most 128 MiB of HBM per device.

```python
import jax
import jax.numpy as jnp
from jax import lax

POINTS = 64
PAIRS_DEV = 16384
LEVELS = 8
PAIRS = 2097152
N_GX = 8
N_GY = 16


def steps_of(rng, extent, split, low, largest):
    loudness = 1.0
    for axis_at, blocks in split:
        heights = jax.random.uniform(jax.random.fold_in(jax.random.fold_in(rng, 6), axis_at), (blocks,), jnp.float32, low / len(split), largest / len(split))
        loudness = loudness * jnp.repeat(jnp.exp(heights), extent[axis_at] // blocks).reshape((-1,) + (1,) * (len(extent) - 1 - axis_at))
    return loudness


def noise(own_key, dims, scale, limit, shards=(), kind=jnp.bfloat16):
    array = scale * jax.random.normal(own_key, dims, jnp.float32)
    if shards:
        array = array * steps_of(own_key, dims, shards, -0.22, 0.18)
    return jnp.clip(array, -limit, limit).astype(kind)


def setup_inputs(seed: int = 0) -> dict:
    key_list = jax.random.split(jax.random.key(seed), 7)
    return {
        "weights": noise(key_list[0], (PAIRS, 2 * POINTS), 1.0, 6.0, ((0, 128),)),
        "travel": jnp.clip(jax.random.uniform(key_list[1], (PAIRS, POINTS), jnp.float32, -3.140625, 3.140625), -3.140625, 3.140625),
        "interp_real": noise(key_list[2], (LEVELS, 2, 2, POINTS, POINTS), (4 * POINTS) ** -0.5, 0.375),
        "interp_imag": noise(key_list[3], (LEVELS, 2, 2, POINTS, POINTS), (4 * POINTS) ** -0.5, 0.375),
        "eval_real": noise(key_list[4], (POINTS, POINTS), (2 * POINTS) ** -0.5, 0.5),
        "eval_imag": noise(key_list[5], (POINTS, POINTS), (2 * POINTS) ** -0.5, 0.5),
    }


def complex_block(part_real, part_imag):
    real_t = part_real.T.astype(jnp.float32)
    imag_t = part_imag.T.astype(jnp.float32)
    upper = jnp.concatenate([real_t, imag_t], 1)
    lower = jnp.concatenate([-imag_t, real_t], 1)
    return jnp.concatenate([upper, lower], 0)


def level_matrix(part_real, part_imag):
    row_blocks = []
    for c_in in range(2):
        col_blocks = []
        for c_out in range(2):
            col_blocks.append(complex_block(part_real[c_out, c_in], part_imag[c_out, c_in]))
        row_blocks.append(jnp.concatenate(col_blocks, 1))
    return jnp.concatenate(row_blocks, 0)


def rotate(values, angle):
    width = angle.shape[-1]
    real_part = values[..., :width]
    imag_part = values[..., width:]
    cosine = jnp.cos(angle)
    sine = jnp.sin(angle)
    return jnp.concatenate([real_part * cosine - imag_part * sine, real_part * sine + imag_part * cosine], -1)


def reference(weights, travel, interp_real, interp_imag, eval_real, eval_imag):
    groups = N_GX * N_GY
    nbits = groups.bit_length() - 1
    half_rows = PAIRS_DEV // 2
    width = 2 * POINTS
    state = weights.reshape(groups, PAIRS_DEV, width)
    phases = travel.reshape(groups, PAIRS_DEV, POINTS)
    for level in range(LEVELS):
        bit_index = level % nbits
        matrix = level_matrix(interp_real[level], interp_imag[level])
        upper_count = groups >> (bit_index + 1)
        lower_count = 1 << bit_index
        blocks = state.reshape(upper_count, 2, lower_count, PAIRS_DEV, width)
        results = []
        for side in range(2):
            first = blocks[:, 0, :, side * half_rows:(side + 1) * half_rows]
            second = blocks[:, 1, :, side * half_rows:(side + 1) * half_rows]
            paired = jnp.concatenate([first, second], -1).astype(jnp.float32)
            mixed = jnp.einsum("abjk,kn->abjn", paired, matrix, precision=lax.Precision.HIGHEST)
            mixed = mixed.reshape(upper_count, lower_count, half_rows, 2, width)
            mixed = jnp.swapaxes(mixed, 2, 3).reshape(upper_count, lower_count, PAIRS_DEV, width)
            results.append(mixed)
        mixed_all = jnp.stack(results, 1).reshape(groups, PAIRS_DEV, width)
        state = rotate(mixed_all, phases * (level + 1.0)).astype(jnp.bfloat16)
    block_rows = PAIRS_DEV // (2 * groups)
    relaid = state.reshape(groups, 2, groups, block_rows, width)
    relaid = jnp.transpose(relaid, (2, 1, 0, 3, 4)).reshape(groups * PAIRS_DEV, width)
    evaluation = complex_block(eval_real, eval_imag)
    image = jnp.dot(relaid.astype(jnp.float32), evaluation, precision=lax.Precision.HIGHEST)
    return image.astype(jnp.bfloat16)
```

```python
import functools

import jax
import jax.numpy as jnp
from jax import lax
from jax.experimental import pallas as pl
from jax.experimental.pallas import tpu as pltpu
from jax.sharding import PartitionSpec as P

LEVELS = 8
GROUPS = 128
HALVES = GROUPS // 2
ROWS = 16
LANES = 128
SCALE = 40.0


def odd_bits(n):
    return bin(n).count("1") % 2


def level_matrices(real, imag):
    def block(kind_in, child_in, kind_out, child_out):
        if kind_in == kind_out:
            return real[child_out, child_in].T
        part = imag[child_out, child_in].T
        return -part if kind_in == 1 else part

    def build(rows, columns):
        return jnp.concatenate(
            [jnp.concatenate([block(*r, *c) for c in columns], 1) for r in rows], 0
        )

    return block, build


KIND_CHILD = [(k, c) for k in range(2) for c in range(2)]
KIND_CHILD_SWAPPED = [(k, 1 - c) for k in range(2) for c in range(2)]
CHILD_KIND = [(k, c) for c in range(2) for k in range(2)]


def all_matrices(interp_real, interp_imag, eval_real, eval_imag):
    mats = []
    for level in range(LEVELS):
        _, build = level_matrices(interp_real[level], interp_imag[level])
        rows_even = CHILD_KIND if level == 0 else KIND_CHILD
        rows_odd = CHILD_KIND if level == 0 else KIND_CHILD_SWAPPED
        mats.append(build(rows_even, KIND_CHILD))
        mats.append(build(rows_odd, KIND_CHILD_SWAPPED))
    zero = jnp.zeros_like(eval_real)
    real = jnp.stack([jnp.stack([eval_real, zero]), jnp.stack([zero, eval_real])])
    imag = jnp.stack([jnp.stack([eval_imag, zero]), jnp.stack([zero, eval_imag])])
    _, build = level_matrices(real, imag)
    mats.append(build(KIND_CHILD, CHILD_KIND))
    mats.append(build(KIND_CHILD_SWAPPED, CHILD_KIND))
    return jnp.stack(mats)


def sine_cosine(angle):
    half = angle * 0.5
    sq = half * half
    sine = half * (1.0 + sq * (-1.6666667e-1 + sq * (8.3333310e-3 + sq * (-1.9840874e-4 + sq * (2.7525562e-6 - 2.3889859e-8 * sq)))))
    cosine = 1.0 + sq * (-0.5 + sq * (4.1666642e-2 + sq * (-1.3888378e-3 + sq * (2.4760495e-5 - 2.6051615e-7 * sq))))
    return 2.0 * sine * cosine, 1.0 - 2.0 * sine * sine


def wave(weights, codes, mats, out, re, im, cos1, sin1, cosl, sinl):
    low = lax.broadcasted_iota(jnp.int32, (ROWS, LANES), 1) < LANES // 2
    flat = lambda tiles: jnp.concatenate(tiles, 0)

    def owner(parity, v):
        return 2 * v + (odd_bits(v) + parity) % 2

    def start(blk, _):
        for parity in range(2):
            for i in range(8):
                v = blk * 8 + i
                odd = (odd_bits(i) + parity) % 2
                flip = lax.rem(blk + blk // 2 + blk // 4, 2)
                d = 2 * v + odd + flip * (1 - 2 * odd)
                angle = jnp.log2(codes(d).astype(jnp.float32)) * (1.0 / SCALE)
                sine, cosine = sine_cosine(angle)
                for ref in (cos1, cosl):
                    ref[parity, v] = cosine
                for ref in (sin1, sinl):
                    ref[parity, v] = sine
        return 0

    lax.fori_loop(0, HALVES // 8, start, 0)

    def rotate_store(mixed, parity, vs, level):
        for k, v in enumerate(vs):
            real = mixed[k * ROWS:(k + 1) * ROWS, :LANES]
            imag = mixed[k * ROWS:(k + 1) * ROWS, LANES:]
            cosine, sine = cosl[parity, v], sinl[parity, v]
            re[parity, v] = (real * cosine - imag * sine).astype(jnp.bfloat16)
            im[parity, v] = (real * sine + imag * cosine).astype(jnp.bfloat16)
            if level < LEVELS - 1:
                c, s = cos1[parity, v], sin1[parity, v]
                cosl[parity, v] = cosine * c - sine * s
                sinl[parity, v] = cosine * s + sine * c

    blocks = 4
    span = HALVES // blocks

    def first(blk, _):
        flip = lax.rem(blk + blk // 2, 2)
        for parity in range(2):
            vs = [blk * span + i for i in range(span)]
            left, right = [], []
            for i, v in enumerate(vs):
                odd = (odd_bits(i) + parity) % 2
                s = odd + flip * (1 - 2 * odd)
                left.append(weights(s, 2 * v))
                right.append(weights(s, 2 * v + 1))
            x = jnp.concatenate([flat(left), flat(right)], 1)
            mixed = jnp.dot(x, mats[parity], preferred_element_type=jnp.float32)
            rotate_store(mixed, parity, vs, 0)
        return 0

    lax.fori_loop(0, blocks, first, 0)

    for level in range(1, LEVELS):
        bit = level % 7 - 1
        step = 0 if bit < 0 else 1 << bit
        if bit < 4:
            base = [i for i in range(span)]
            stride = span
        else:
            base = [i + 8 * 0 for i in range(8)] + [i + (1 << bit) for i in range(8)]
            stride = None

        def body(blk, _, level=level, bit=bit, step=step, base=base, stride=stride):
            if stride is not None:
                offset = blk * stride
            elif bit == 4:
                offset = lax.rem(blk, 2) * 8 + blk // 2 * 32
            else:
                offset = blk * 8
            sel = [[], []]
            vs = [offset + i for i in base]
            ws = [offset + (i ^ step) for i in base]
            pieces = [[[], []], [[], []]]
            if bit < 0:
                flip = lax.rem(blk + blk // 2, 2)
                masks = [low != (flip == 1), low == (flip == 1)]
            for i, v, w in zip(base, vs, ws):
                if bit < 0:
                    mask = masks[odd_bits(i)]
                else:
                    mask = low if (i >> bit) % 2 == 0 else jnp.logical_not(low)
                for kind, ref in enumerate((re, im)):
                    even, odd = ref[0, v], ref[1, w]
                    pieces[0][kind].append(jnp.where(mask, even, odd))
                    pieces[1][kind].append(jnp.where(mask, odd, even))
            mixed = []
            for parity in range(2):
                x = jnp.concatenate([flat(pieces[parity][0]), flat(pieces[parity][1])], 1)
                mixed.append(jnp.dot(x, mats[2 * level + parity], preferred_element_type=jnp.float32))
            for parity in range(2):
                rotate_store(mixed[parity], parity, (vs, ws)[parity], level)
            return 0

        lax.fori_loop(0, blocks, body, 0)

    def last(blk, _):
        flip = lax.rem(blk + blk // 2, 2)
        for parity in range(2):
            vs = [blk * span + i for i in range(span)]
            x = jnp.concatenate([flat([re[parity, v] for v in vs]), flat([im[parity, v] for v in vs])], 1)
            image = jnp.dot(x, mats[2 * LEVELS + parity], preferred_element_type=jnp.float32).astype(jnp.bfloat16)
            for i, v in enumerate(vs):
                odd = (odd_bits(i) + parity) % 2
                d = 2 * v + odd + flip * (1 - 2 * odd)
                for s in range(2):
                    out[s, d] = image[i * ROWS:(i + 1) * ROWS, s * LANES:(s + 1) * LANES]
        return 0

    lax.fori_loop(0, blocks, last, 0)


def compute_kernel(arrived, mats, out, *scratch):
    wave(lambda s, d: arrived[s, d], lambda d: arrived[2, d], mats, out, *scratch)


def wave_scratch():
    state = pltpu.VMEM((2, HALVES, ROWS, LANES), jnp.bfloat16)
    phase = pltpu.VMEM((2, HALVES, ROWS, LANES), jnp.float32)
    return [state, state, phase, phase, phase, phase]


def local(weights, travel, interp_real, interp_imag, eval_real, eval_imag):
    pair_rows, width = weights.shape
    block_rows = pair_rows // (2 * GROUPS)
    me = lax.axis_index(("gx", "gy"))
    odd = lax.rem(lax.population_count(me), 2)
    phases = travel.reshape(2, GROUPS, block_rows, width // 2)
    phases = jnp.where(odd == 1, phases[::-1], phases)
    codes = jnp.exp2(SCALE * jnp.concatenate([phases[0], phases[1]], -1)).astype(jnp.bfloat16)
    sent = jnp.concatenate([weights.reshape(2, GROUPS, block_rows, width), codes[None]], 0)
    arrived = lax.all_to_all(sent, ("gx", "gy"), split_axis=1, concat_axis=1, tiled=True)
    mats = all_matrices(interp_real, interp_imag, eval_real, eval_imag)
    image = pl.pallas_call(
        compute_kernel,
        grid=(block_rows // ROWS,),
        in_specs=[
            pl.BlockSpec((3, GROUPS, ROWS, LANES), lambda w: (0, 0, w, 0)),
            pl.BlockSpec(mats.shape, lambda w: (0, 0, 0)),
        ],
        out_specs=pl.BlockSpec((2, GROUPS, ROWS, LANES), lambda w: (0, 0, w, 0)),
        out_shape=jax.ShapeDtypeStruct((2, GROUPS, block_rows, width), jnp.bfloat16),
        scratch_shapes=wave_scratch(),
        compiler_params=pltpu.CompilerParams(vmem_limit_bytes=40 << 20),
    )(arrived, mats)
    return image.reshape(pair_rows, width)


def solution(mesh):
    return jax.shard_map(
        local,
        mesh=mesh,
        in_specs=(P(("gx", "gy"), None), P(("gx", "gy"), None), P(), P(), P(), P()),
        out_specs=P(("gx", "gy"), None),
        check_vma=False,
    )
```

```python
import jax
import jax.numpy as jnp
from jax import lax
from jax.experimental import pallas as pl
from jax.experimental.pallas import tpu as pltpu
from jax.sharding import PartitionSpec as P

MESH = pl.DeviceIdType.MESH
LEVELS = 8
GROUPS = 128
HALVES = GROUPS // 2
ROWS = 16
WAVES = 4
LANES = 128
HALF = LANES // 2
SPAN = 16
SCALE = 40.0
DIGITS = (2, 4, 4, 4)
CODES = 2
ORDERS = (("xyz", "yzx", "zxy"), ("zxy", "xyz", "yzx"), ("xyz", "yzx", "zxy"), ("xyz", "yzx", "zxy"))


def odd_bits(n):
    return bin(n).count("1") % 2


def digits(d):
    return d // 64, d // 16 % 4, d // 4 % 4, d % 4


def owner(parity, v):
    return 2 * v + (odd_bits(v) + parity) % 2


def sine_cosine(angle):
    half = angle * 0.5
    sq = half * half
    sine = half * (1.0 + sq * (-1.6666667e-1 + sq * (8.3333310e-3 + sq * (-1.9840874e-4 + sq * (2.7525562e-6 - 2.3889859e-8 * sq)))))
    cosine = 1.0 + sq * (-0.5 + sq * (4.1666642e-2 + sq * (-1.3888378e-3 + sq * (2.4760495e-5 - 2.6051615e-7 * sq))))
    twice = 2.0 * sine
    return twice * cosine, 1.0 - twice * sine


def build_matrices(real, imag, eval_real, eval_imag, mats):
    flip = lambda parity, child: (child + parity) % 2

    def halves(level):
        tr = [[real[level, c, e].astype(jnp.float32).T for e in range(2)] for c in range(2)]
        ti = [[imag[level, c, e].astype(jnp.float32).T for e in range(2)] for c in range(2)]

        def rows(kind, e, parity):
            a, b = flip(parity, 0), flip(parity, 1)
            if kind == 0:
                parts = [tr[a][e], tr[b][e], ti[a][e], ti[b][e]]
            else:
                parts = [-ti[a][e], -ti[b][e], tr[a][e], tr[b][e]]
            return jnp.concatenate(parts, 1).astype(jnp.bfloat16)

        return rows

    rows = halves(0)
    for parity in range(2):
        for e in range(2):
            for kind in range(2):
                mats[parity, (2 * e + kind) * HALF:(2 * e + kind + 1) * HALF] = rows(kind, e, parity)

    def level_body(level, _):
        rows = halves(level)
        for parity in range(2):
            for kind in range(2):
                for e in range(2):
                    at = 2 * kind + flip(parity, e)
                    mats[2 * level + parity, at * HALF:(at + 1) * HALF] = rows(kind, e, parity)
        return 0

    lax.fori_loop(1, LEVELS, level_body, 0)
    er = eval_real[...].astype(jnp.float32).T
    ei = eval_imag[...].astype(jnp.float32).T
    both = [jnp.concatenate([er, ei], 1).astype(jnp.bfloat16), jnp.concatenate([-ei, er], 1).astype(jnp.bfloat16)]
    zero = jnp.zeros((HALF, LANES), jnp.bfloat16)
    for parity in range(2):
        for kind in range(2):
            for c in range(2):
                at = 2 * kind + flip(parity, c)
                line = [both[kind], zero] if c == 0 else [zero, both[kind]]
                mats[2 * LEVELS + parity, at * HALF:(at + 1) * HALF] = jnp.concatenate(line, 1)


def times(a, b):
    return a[0] * b[0] - a[1] * b[1], a[0] * b[1] + a[1] * b[0]


def wave(weights, codes, mats, put, re, im, powers):
    low = lax.broadcasted_iota(jnp.int32, (ROWS, LANES), 1) < HALF
    high = jnp.logical_not(low)
    flat = lambda tiles: jnp.concatenate(tiles, 0)

    def phase(level, parity, v):
        load = lambda i: (powers[i, 0, parity, v], powers[i, 1, parity, v])

        def keep(i, value):
            powers[i, 0, parity, v], powers[i, 1, parity, v] = value
            return value

        if level == 0:
            angle = jnp.log2(codes(owner(parity, v)).astype(jnp.float32)) * (1.0 / SCALE)
            sine, cosine = sine_cosine(angle)
            return keep(0, (cosine, sine))
        if level == 1:
            cosine, sine = load(0)
            twice = 2.0 * sine
            return keep(1, (1.0 - twice * sine, twice * cosine))
        if level == 2:
            return keep(2, times(load(1), load(0)))
        if level == 3:
            cosine, sine = load(1)
            twice = 2.0 * sine
            return keep(3, (1.0 - twice * sine, twice * cosine))
        if level == 7:
            cosine, sine = load(3)
            twice = 2.0 * sine
            return 1.0 - twice * sine, twice * cosine
        return times(load(3), load(level - 4))

    def rotate_store(mixed, parity, vs, level):
        for k, v in enumerate(vs):
            real = mixed[k * ROWS:(k + 1) * ROWS, :LANES]
            imag = mixed[k * ROWS:(k + 1) * ROWS, LANES:]
            cosine, sine = phase(level, parity, v)
            re[parity, v] = (real * cosine - imag * sine).astype(jnp.bfloat16)
            im[parity, v] = (real * sine + imag * cosine).astype(jnp.bfloat16)

    for blk in range(HALVES // SPAN):
        vs = range(blk * SPAN, (blk + 1) * SPAN)
        for parity in range(2):
            left = [weights((odd_bits(v) + parity) % 2, 2 * v) for v in vs]
            right = [weights((odd_bits(v) + parity) % 2, 2 * v + 1) for v in vs]
            x = jnp.concatenate([flat(left), flat(right)], 1)
            mixed = jnp.dot(x, mats[parity], preferred_element_type=jnp.float32)
            rotate_store(mixed, parity, vs, 0)

    for level in range(1, LEVELS):
        bit = level % 7 - 1
        step = 0 if bit < 0 else 1 << bit
        for blk in range(HALVES // SPAN):
            vs = list(range(blk * SPAN, (blk + 1) * SPAN))
            ws = [v ^ step for v in vs]
            pieces = [[[], []], [[], []]]
            for v, w in zip(vs, ws):
                second = odd_bits(v) if bit < 0 else v >> bit & 1
                mask = high if second else low
                for kind, ref in enumerate((re, im)):
                    even, odd = ref[0, v], ref[1, w]
                    pieces[0][kind].append(jnp.where(mask, even, odd))
                    pieces[1][kind].append(jnp.where(mask, odd, even))
            for parity in range(2):
                x = jnp.concatenate([flat(pieces[parity][0]), flat(pieces[parity][1])], 1)
                mixed = jnp.dot(x, mats[2 * level + parity], preferred_element_type=jnp.float32)
                rotate_store(mixed, parity, (vs, ws)[parity], level)

    for blk in range(HALVES // SPAN):
        vs = range(blk * SPAN, (blk + 1) * SPAN)
        for parity in range(2):
            x = jnp.concatenate([flat([re[parity, v] for v in vs]), flat([im[parity, v] for v in vs])], 1)
            image = jnp.dot(x, mats[2 * LEVELS + parity], preferred_element_type=jnp.float32).astype(jnp.bfloat16)
            for i, v in enumerate(vs):
                for s in range(2):
                    put(s, owner(parity, v), image[i * ROWS:(i + 1) * ROWS, s * LANES:(s + 1) * LANES])


def kernel(
    weights, travel, interp_real, interp_imag, eval_real, eval_imag, image,
    held, coded, angles, reals, imags, er, ei, mats, re, im, powers,
    send_sem, recv_sem, load_sem,
):
    gx, gy = lax.axis_index("gx"), lax.axis_index("gy")
    xh, z, y, u = gx // 4, gx % 4, gy // 4, gy % 4
    bits = xh + z + z // 2 + y + y // 2 + u + u // 2
    odd = bits % 2

    loads = [
        pltpu.make_async_copy(travel.at[:, pl.ds(0, 8192)], angles.at[odd], load_sem.at[0]),
        pltpu.make_async_copy(travel.at[:, pl.ds(8192, 8192)], angles.at[1 - odd], load_sem.at[1]),
        pltpu.make_async_copy(interp_real, reals, load_sem.at[2]),
        pltpu.make_async_copy(interp_imag, imags, load_sem.at[3]),
        pltpu.make_async_copy(eval_real, er, load_sem.at[4]),
        pltpu.make_async_copy(eval_imag, ei, load_sem.at[5]),
    ]
    for load in loads:
        load.start()

    def peer(axis, k):
        if axis == "x":
            p = (xh * 4 + u + k) % 8
            return (p // 4, p % 4), (p // 4 * 4 + z, y * 4 + p % 4)
        if axis == "y":
            p = (y + k) % 4
            return (p,), (gx, p * 4 + u)
        p = (z + k) % 4
        return (p,), (xh * 4 + p, gy)

    def part(axis, at):
        if axis == "x":
            return at[0], slice(None), slice(None), at[1]
        if axis == "y":
            return slice(None), slice(None), at[0]
        return slice(None), at[0]

    def count(axis):
        return 8 if axis == "x" else 4

    barrier = pltpu.get_barrier_semaphore()
    for axis in "xyz":
        def greet(k, _, axis=axis):
            pl.semaphore_signal(barrier, inc=1, device_id=peer(axis, k)[1], device_id_type=MESH)
            return 0
        lax.fori_loop(1, count(axis), greet, 0)
    pl.semaphore_wait(barrier, 13)

    def start(stage, stream, w):
        axis = ORDERS[w][stream][stage]
        if stage > 0:
            source = lambda at: held.at[(stage - 1, stream, w) + part(axis, at)]
        elif stream == CODES:
            source = lambda at: coded.at[(w,) + part(axis, at)]
        else:
            def source(at):
                index = part(axis, at)
                index = index + (slice(None),) * (4 - len(index))
                return weights.at[(stream,) + index + (pl.ds(w * ROWS, ROWS),)]
        mine = peer(axis, 0)[0]
        target = held.at[(stage, stream, w) + part(axis, mine)]

        def send(k, _):
            at, device = peer(axis, k)
            pltpu.make_async_remote_copy(
                src_ref=source(at), dst_ref=target,
                send_sem=send_sem.at[stage, stream, w], recv_sem=recv_sem.at[stage, stream, w],
                device_id=device, device_id_type=MESH,
            ).start()
            return 0

        lax.fori_loop(1, count(axis), send, 0)
        pltpu.make_async_copy(source(mine), target, recv_sem.at[stage, stream, w]).start()

    def land(stage, stream, w):
        whole = held.at[stage, stream, w]
        pltpu.make_async_copy(whole, whole, recv_sem.at[stage, stream, w]).wait()

    for w in range(2):
        for stream in range(2):
            start(0, stream, w)

    loads[0].wait()
    loads[1].wait()

    def encode(hz, _):
        for low in range(8):
            at = pl.ds(pl.multiple_of((hz * 8 + low) * LANES, LANES), LANES)
            both = jnp.concatenate([angles[0, :, at], angles[1, :, at]], 0)
            code = jnp.exp2(SCALE * both).T.astype(jnp.bfloat16)
            for h in range(2):
                for w in range(WAVES):
                    row = h * 64 + w * ROWS
                    coded[w, hz // 4, hz % 4, low // 2, low % 2 * 2 + h] = code[row:row + ROWS]
        return 0

    lax.fori_loop(0, 8, encode, 0)
    for w in range(2):
        start(0, CODES, w)

    streams = range(3)
    for stream in streams:
        land(0, stream, 0)
        start(1, stream, 0)
    for stream in streams:
        land(0, stream, 1)
        start(1, stream, 1)
    for w in range(2):
        for stream in streams:
            land(1, stream, w)
            start(2, stream, w)
        for stream in streams:
            start(0, stream, w + 2)
    for load in loads[2:]:
        load.wait()
    build_matrices(reals, imags, er, ei, mats)

    def step(w, _):
        for stream in streams:
            whole = held.at[2, stream, w]
            pltpu.make_async_copy(whole, whole, recv_sem.at[2, stream, w]).wait()

        def put(s, d, value):
            image[s, d, pl.ds(pl.multiple_of(w * ROWS, ROWS), ROWS)] = value

        wave(
            lambda s, d: held[(2, s, w) + digits(d)], lambda d: held[(2, CODES, w) + digits(d)],
            mats, put, re, im, powers,
        )

        @pl.when(w == 0)
        def _():
            for stream in streams:
                land(0, stream, 2)
                start(1, stream, 2)

        @pl.when(w == 1)
        def _():
            for stream in streams:
                land(0, stream, 3)
                start(1, stream, 3)
            for later in (2, 3):
                for stream in streams:
                    land(1, stream, later)
                    start(2, stream, later)
        return 0

    lax.fori_loop(0, WAVES, step, 0)

    for w in range(WAVES):
        for stream in streams:
            for stage in range(3):
                sent = GROUPS - GROUPS // count(ORDERS[w][stream][stage])
                bytes_of = image.at[0, pl.ds(0, sent), pl.ds(0, ROWS)]
                pltpu.make_async_copy(bytes_of, bytes_of, send_sem.at[stage, stream, w]).wait()


def local(weights, travel, interp_real, interp_imag, eval_real, eval_imag):
    pair_rows, width = weights.shape
    block_rows = pair_rows // (2 * GROUPS)
    bf16, f32 = jnp.bfloat16, jnp.float32
    image = pl.pallas_call(
        kernel,
        in_specs=[pl.BlockSpec(memory_space=pl.ANY)] * 6,
        out_specs=pl.BlockSpec(memory_space=pltpu.VMEM),
        out_shape=pltpu.VMEM((2, GROUPS, block_rows, width), bf16),
        scratch_shapes=[
            pltpu.VMEM((3, 3, WAVES) + DIGITS + (ROWS, LANES), bf16),
            pltpu.VMEM((WAVES,) + DIGITS + (ROWS, LANES), bf16),
            pltpu.VMEM((2, HALF, pair_rows // 2), f32),
            pltpu.VMEM(interp_real.shape, bf16),
            pltpu.VMEM(interp_imag.shape, bf16),
            pltpu.VMEM(eval_real.shape, bf16),
            pltpu.VMEM(eval_imag.shape, bf16),
            pltpu.VMEM((2 * LEVELS + 2, 2 * LANES, 2 * LANES), bf16),
            pltpu.VMEM((2, HALVES, ROWS, LANES), bf16),
            pltpu.VMEM((2, HALVES, ROWS, LANES), bf16),
            pltpu.VMEM((4, 2, 2, HALVES, ROWS, LANES), f32),
            pltpu.SemaphoreType.DMA((3, 3, WAVES)),
            pltpu.SemaphoreType.DMA((3, 3, WAVES)),
            pltpu.SemaphoreType.DMA((6,)),
        ],
        compiler_params=pltpu.CompilerParams(
            collective_id=0, has_side_effects=True, vmem_limit_bytes=56 << 20
        ),
    )(weights.reshape((2,) + DIGITS + (block_rows, width)), travel.T, interp_real, interp_imag, eval_real, eval_imag)
    return image.reshape(pair_rows, width)


def solution(mesh):
    return jax.shard_map(
        local,
        mesh=mesh,
        in_specs=(P(("gx", "gy"), None), P(("gx", "gy"), None), P(), P(), P(), P()),
        out_specs=P(("gx", "gy"), None),
        check_vma=False,
    )
```

```python
import functools

import jax
import jax.numpy as jnp
from jax import lax
from jax.experimental import pallas as pl
from jax.experimental.pallas import tpu as pltpu
from jax.sharding import PartitionSpec as P

MESH = pl.DeviceIdType.MESH
LEVELS = 8
GROUPS = 128
HALVES = GROUPS // 2
ROWS = 16
WAVES = 4
LANES = 128
HALF = LANES // 2
SPAN = 16
SCALE = 40.0
DECODE = 0.018033688011112043
DIGITS = (2, 4, 4, 4)
CODES = 2
GROUPED = (
    ((0, 0), (1, 0), (2, 0)),
    ((2, 1), (2, 2), (2, 3)),
    ((0, 1), (1, 1), (0, 2)),
    ((1, 2), (0, 3), (1, 3)),
)
SLOTS = 3


def axis_of(place, stage):
    return "xyz"[(place + stage) % 3]


def odd_bits(n):
    return bin(n).count("1") % 2


def digits(d):
    return d // 64, d // 16 % 4, d // 4 % 4, d % 4


def double(a):
    twice = a[1] + a[1]
    return 1.0 - twice * a[1], twice * a[0]


def next_odd(twice, even, odd):
    return twice * even[0] - odd[0], twice * even[1] - odd[1]


def unit(half):
    sq = half * half
    sine = half * (0.999999977 + sq * (-1.66666476e-1 + sq * (8.33289965e-3 + sq * (-1.98008872e-4 + sq * 2.59046704e-6))))
    cosine = 0.99999995 + sq * (-0.49999905 + sq * (4.16635835e-2 + sq * (-1.38536951e-3 + sq * 2.3153718e-5)))
    return double((cosine, sine))


def build_matrices(real, imag, eval_real, eval_imag, mats):
    flip = lambda parity, child: (child + parity) % 2

    def blocks_of(level):
        tr = [[real[level, c, e].astype(jnp.float32).T for e in range(2)] for c in range(2)]
        ti = [[imag[level, c, e].astype(jnp.float32).T for e in range(2)] for c in range(2)]

        def rows(kind, e, parity):
            a, b = flip(parity, 0), flip(parity, 1)
            if kind == 0:
                parts = [tr[a][e], tr[b][e], ti[a][e], ti[b][e]]
            else:
                parts = [-ti[a][e], -ti[b][e], tr[a][e], tr[b][e]]
            return jnp.concatenate(parts, 1).astype(jnp.bfloat16)

        return rows

    rows = blocks_of(0)
    for parity in range(2):
        for e in range(2):
            for kind in range(2):
                mats[parity, (2 * e + kind) * HALF:(2 * e + kind + 1) * HALF] = rows(kind, e, parity)

    def level_body(level, _):
        rows = blocks_of(level)
        for parity in range(2):
            for kind in range(2):
                for e in range(2):
                    at = 2 * kind + flip(parity, e)
                    mats[2 * level + parity, at * HALF:(at + 1) * HALF] = rows(kind, e, parity)
        return 0

    lax.fori_loop(1, LEVELS, level_body, 0)
    er = eval_real[...].astype(jnp.float32).T
    ei = eval_imag[...].astype(jnp.float32).T
    both = [jnp.concatenate([er, ei], 1).astype(jnp.bfloat16), jnp.concatenate([-ei, er], 1).astype(jnp.bfloat16)]
    zero = jnp.zeros((HALF, LANES), jnp.bfloat16)
    for parity in range(2):
        for kind in range(2):
            for c in range(2):
                at = 2 * kind + flip(parity, c)
                line = [both[kind], zero] if c == 0 else [zero, both[kind]]
                mats[2 * LEVELS + parity, at * HALF:(at + 1) * HALF] = jnp.concatenate(line, 1)


def tables(codes, powers):
    def body(blk, _):
        turn = lax.rem(blk + blk // 2 + blk // 4, 2)
        for s in range(2):
            for parity in range(2):
                for y in range(4):
                    k = blk * 4 + y
                    e = odd_bits(y) ^ parity ^ s
                    u = 2 * (e + turn * (1 - 2 * e)) + s
                    one = unit(jnp.log(codes(blk, y, u).astype(jnp.float32)) * DECODE)
                    twice = one[0] + one[0]
                    two = double(one)
                    three = next_odd(twice, two, one)
                    four = double(two)
                    five = next_odd(twice, four, three)
                    six = double(three)
                    all_powers = (one, two, three, four, five, six, next_odd(twice, six, five), double(four))
                    for n, value in enumerate(all_powers):
                        for i in range(2):
                            powers[n, i, s, parity, k] = value[i].astype(jnp.bfloat16)
        return 0

    lax.fori_loop(0, 8, body, 0)


def rotate(mixed, powers, level, at, re, im):
    mixed = mixed.astype(jnp.bfloat16)
    real = mixed[:, :LANES].reshape(SPAN, ROWS, LANES)
    imag = mixed[:, LANES:].reshape(SPAN, ROWS, LANES)
    cosine, sine = powers[(level, 0) + at], powers[(level, 1) + at]
    re[at] = real * cosine - imag * sine
    im[at] = real * sine + imag * cosine


def low_lanes(tiles=None):
    shape = (ROWS, LANES) if tiles is None else (tiles, ROWS, LANES)
    return lax.broadcasted_iota(jnp.int32, shape, len(shape) - 1) < HALF


def flat(tiles):
    return jnp.concatenate(tiles, 0)


def rows(tiles):
    return tiles.reshape(SPAN * ROWS, LANES)


def multiply(real, imag, matrix):
    return jnp.dot(jnp.concatenate([real, imag], 1), matrix, preferred_element_type=jnp.float32)


def combine(even, odd, take, mats, level, powers, re, im):
    pieces = [take(ref[even], ref[odd]) for ref in (re, im)]
    for parity, at in enumerate((even, odd)):
        mixed = multiply(rows(pieces[0][parity]), rows(pieces[1][parity]), mats[2 * level + parity])
        rotate(mixed, powers, level, at, re, im)


def swap(mask):
    return lambda even, odd: (jnp.where(mask, even, odd), jnp.where(mask, odd, even))


def halves(tiles, step):
    parts = tiles.reshape(SPAN // (2 * step), 2, step, ROWS, LANES)
    return [parts[:, n].reshape(SPAN // 2, ROWS, LANES) for n in range(2)]


def whole(parts, step):
    shape = (SPAN // (2 * step), 1, step, ROWS, LANES)
    return jnp.concatenate([p.reshape(shape) for p in parts], 1).reshape(SPAN, ROWS, LANES)


def swap_across(step, low):
    def take(even, odd):
        high = jnp.logical_not(low)
        even, odd = halves(even, step), halves(odd, step)
        return (
            whole([jnp.where(low, even[0], odd[1]), jnp.where(high, even[1], odd[0])], step),
            whole([jnp.where(high, odd[0], even[1]), jnp.where(low, odd[1], even[0])], step),
        )

    return take


def chain(s, weights, mats, powers, re, im):
    low = low_lanes()
    if isinstance(s, int):
        turned = jnp.logical_not(low) if s else low
    else:
        turned = jnp.logical_xor(low, jnp.broadcast_to(s == 1, low.shape))
    starts = range(0, GROUPS // 4, SPAN)
    span = lambda at: pl.ds(at, SPAN)

    def first():
        for at in starts:
            for parity in range(2):
                left, right = [], []
                for k in range(at, at + SPAN):
                    bit = s if odd_bits(k) ^ parity == 0 else 1 - s
                    left.append(weights(k // 4, k % 4, 2 * bit))
                    right.append(weights(k // 4, k % 4, 2 * bit + 1))
                rotate(multiply(flat(left), flat(right), mats[parity]), powers, 0, (s, parity, span(at)), re, im)

    def later(level):
        step = 1 << level - 2 if level > 1 else 0

        def second(even, odd):
            masks = [jnp.logical_not(turned) if odd_bits(k) else turned for k in range(SPAN)]
            if starts_odd:
                masks = [jnp.logical_not(m) for m in masks]
            return (
                jnp.stack([jnp.where(m, even[k], odd[k]) for k, m in enumerate(masks)]),
                jnp.stack([jnp.where(m, odd[k], even[k]) for k, m in enumerate(masks)]),
            )

        for at in starts:
            starts_odd = odd_bits(at)
            if level == 1:
                take = second
            elif step < SPAN:
                take = swap_across(step, low_lanes(SPAN // 2))
            else:
                wide = low_lanes(SPAN)
                take = swap(jnp.logical_not(wide) if at & step else wide)
            other = at ^ step if step >= SPAN else at
            combine((s, 0, span(at)), (s, 1, span(other)), take, mats, level, powers, re, im)

    return [first] + [functools.partial(later, level) for level in range(1, LEVELS - 1)]


def together(*chains):
    for levels in zip(*chains):
        for level in levels:
            level()


def joint(mats, powers, re, im, put):
    low = low_lanes(SPAN)
    for s in range(2):
        take = swap(jnp.logical_not(low) if s else low)
        for at in range(0, GROUPS // 4, SPAN):
            ks = pl.ds(at, SPAN)
            combine((s, 0, ks), (1 - s, 1, ks), take, mats, LEVELS - 1, powers, re, im)
    for s in range(2):
        for parity in range(2):
            for at in range(0, GROUPS // 4, SPAN):
                place = (s, parity, pl.ds(at, SPAN))
                image = multiply(rows(re[place]), rows(im[place]), mats[2 * LEVELS + parity]).astype(jnp.bfloat16)
                for n in range(SPAN):
                    k = at + n
                    for c in range(2):
                        put(
                            c, 4 * k + 2 * (odd_bits(k) ^ parity ^ s) + s,
                            image[n * ROWS:(n + 1) * ROWS, c * LANES:(c + 1) * LANES],
                        )


def kernel(
    weights, travel, interp_real, interp_imag, eval_real, eval_imag, image,
    held, coded, angles, reals, imags, er, ei, mats, re, im, powers,
    send_sem, recv_sem, load_sem,
):
    gx, gy = lax.axis_index("gx"), lax.axis_index("gy")
    xh, z, y, u = gx // 4, gx % 4, gy // 4, gy % 4
    bits = xh + z + z // 2 + y + y // 2 + u + u // 2
    odd = bits % 2

    loads = [
        pltpu.make_async_copy(travel.at[:, pl.ds(0, 8192)], angles.at[odd], load_sem.at[0]),
        pltpu.make_async_copy(travel.at[:, pl.ds(8192, 8192)], angles.at[1 - odd], load_sem.at[1]),
        pltpu.make_async_copy(interp_real, reals, load_sem.at[2]),
        pltpu.make_async_copy(interp_imag, imags, load_sem.at[3]),
        pltpu.make_async_copy(eval_real, er, load_sem.at[4]),
        pltpu.make_async_copy(eval_imag, ei, load_sem.at[5]),
    ]
    for load in loads:
        load.start()

    def peer(axis, k):
        if axis == "x":
            x = (xh * 2 + u // 2 + k // 2) % 4
            to = x % 2 * 2 + (u + k) % 2
            return (x // 2, to), (x // 2 * 4 + z, y * 4 + to)
        if axis == "y":
            p = (y + k) % 4
            return (p,), (gx, p * 4 + u)
        p = (z + k) % 4
        return (p,), (xh * 4 + p, gy)

    def part(axis, at):
        if axis == "x":
            return at[0], slice(None), slice(None), at[1]
        if axis == "y":
            return slice(None), slice(None), at[0]
        return slice(None), at[0]

    def count(axis):
        return 8 if axis == "x" else 4

    barrier = pltpu.get_barrier_semaphore()
    for axis in "xyz":
        def greet(k, _, axis=axis):
            pl.semaphore_signal(barrier, inc=1, device_id=peer(axis, k)[1], device_id_type=MESH)
            return 0
        lax.fori_loop(1, count(axis), greet, 0)
    pl.semaphore_wait(barrier, 13)

    def go(group, stage):
        items = GROUPED[group]
        sends = {}
        for place, (stream, w) in enumerate(items):
            if stage > 0:
                land(stage - 1, stream, w)
            sends[axis_of(place, stage)] = one(stage, stream, w, axis_of(place, stage))

        def send(i, _):
            k = 2 + i - i // 2 * 3
            sends["x"][0](2 * k)
            sends["y"][0](k)
            sends["z"][0](k)
            sends["x"][0](2 * k + 1)
            return 0

        lax.fori_loop(0, 3, send, 0)
        sends["x"][0](1)
        for axis in "xyz":
            sends[axis][1]()

    def one(stage, stream, w, axis):
        if stage > 0:
            source = lambda at: held.at[(stage - 1, stream, w) + part(axis, at)]
        elif stream == CODES:
            source = lambda at: coded.at[(w,) + part(axis, at)]
        else:
            def source(at):
                index = part(axis, at)
                index = index + (slice(None),) * (4 - len(index))
                return weights.at[(stream,) + index + (pl.ds(w * ROWS, ROWS),)]
        mine = peer(axis, 0)[0]
        target = held.at[(stage, stream, w) + part(axis, mine)]

        def send(k):
            at, device = peer(axis, k)
            pltpu.make_async_remote_copy(
                src_ref=source(at), dst_ref=target,
                send_sem=send_sem.at[stage, stream, w], recv_sem=recv_sem.at[stage, stream, w],
                device_id=device, device_id_type=MESH,
            ).start()

        def keep():
            pltpu.make_async_copy(source(mine), target, recv_sem.at[stage, stream, w]).start()

        return send, keep

    def land(stage, stream, w):
        whole = held.at[stage, stream, w]
        pltpu.make_async_copy(whole, whole, recv_sem.at[stage, stream, w]).wait()

    go(2, 0)
    go(3, 0)

    loads[0].wait()
    loads[1].wait()

    def encode(hz, _):
        for low in range(8):
            at = pl.ds(pl.multiple_of((hz * 8 + low) * LANES, LANES), LANES)
            both = jnp.concatenate([angles[0, :, at], angles[1, :, at]], 0)
            code = jnp.exp2(SCALE * both).astype(jnp.bfloat16).T
            for h in range(2):
                for w in range(WAVES):
                    row = h * 64 + w * ROWS
                    coded[w, hz // 4, hz % 4, low // 2, low % 2 * 2 + h] = code[row:row + ROWS]
        return 0

    lax.fori_loop(0, 8, encode, 0)
    go(0, 0)
    go(1, 0)
    go(0, 1)
    go(1, 1)
    go(0, 2)
    for load in loads[2:]:
        load.wait()
    build_matrices(reals, imags, er, ei, mats)
    go(1, 2)
    go(2, 1)
    go(3, 1)

    def tabulate(w):
        land(2, CODES, w)
        tables(lambda blk, y, u: held[2, CODES, w, blk // 4, blk % 4, y, u], powers.at[w % SLOTS])

    tabulate(0)

    def links(s, w, state):
        return chain(
            s, lambda xz, y, u: held[2, s, w, xz // 4, xz % 4, y, u], mats, powers.at[w % SLOTS], *state
        )

    def finish(w, state):
        def put(c, d, value):
            image[c, d, pl.ds(pl.multiple_of(w * ROWS, ROWS), ROWS)] = value

        joint(mats, powers.at[w % SLOTS], *state, put)

    near, far = (re.at[0], im.at[0]), (re.at[1], im.at[1])
    land(2, 0, 0)
    land(2, 1, 0)

    def side(s, _):
        together(links(s, 0, near))
        return 0

    lax.fori_loop(0, 2, side, 0)
    finish(0, near)
    tabulate(1)
    go(2, 2)
    tabulate(2)
    go(3, 2)
    tabulate(3)

    def step(t, _):
        w = 1 + 2 * t
        land(2, 0, w)
        land(2, 1, w)
        land(2, t, 2)
        together(links(0, w, near), links(1, w, near), links(t, 2, far))
        finish(w, near)
        return 0

    lax.fori_loop(0, 2, step, 0)
    finish(2, far)

    for items in GROUPED:
        for place, (stream, w) in enumerate(items):
            for stage in range(3):
                sent = GROUPS - GROUPS // count(axis_of(place, stage))
                bytes_of = image.at[0, pl.ds(0, sent), pl.ds(0, ROWS)]
                pltpu.make_async_copy(bytes_of, bytes_of, send_sem.at[stage, stream, w]).wait()


def local(weights, travel, interp_real, interp_imag, eval_real, eval_imag):
    pair_rows, width = weights.shape
    block_rows = pair_rows // (2 * GROUPS)
    bf16, f32 = jnp.bfloat16, jnp.float32
    image = pl.pallas_call(
        kernel,
        in_specs=[pl.BlockSpec(memory_space=pl.ANY)] * 6,
        out_specs=pl.BlockSpec(memory_space=pltpu.VMEM),
        out_shape=pltpu.VMEM((2, GROUPS, block_rows, width), bf16),
        scratch_shapes=[
            pltpu.VMEM((3, 3, WAVES) + DIGITS + (ROWS, LANES), bf16),
            pltpu.VMEM((WAVES,) + DIGITS + (ROWS, LANES), bf16),
            pltpu.VMEM((2, HALF, pair_rows // 2), f32),
            pltpu.VMEM(interp_real.shape, bf16),
            pltpu.VMEM(interp_imag.shape, bf16),
            pltpu.VMEM(eval_real.shape, bf16),
            pltpu.VMEM(eval_imag.shape, bf16),
            pltpu.VMEM((2 * LEVELS + 2, 2 * LANES, 2 * LANES), bf16),
            pltpu.VMEM((2, 2, 2, GROUPS // 4, ROWS, LANES), bf16),
            pltpu.VMEM((2, 2, 2, GROUPS // 4, ROWS, LANES), bf16),
            pltpu.VMEM((SLOTS, LEVELS, 2, 2, 2, GROUPS // 4, ROWS, LANES), bf16),
            pltpu.SemaphoreType.DMA((3, 3, WAVES)),
            pltpu.SemaphoreType.DMA((3, 3, WAVES)),
            pltpu.SemaphoreType.DMA((6,)),
        ],
        compiler_params=pltpu.CompilerParams(
            collective_id=0, has_side_effects=True, vmem_limit_bytes=56 << 20
        ),
    )(weights.reshape((2,) + DIGITS + (block_rows, width)), travel.T, interp_real, interp_imag, eval_real, eval_imag)
    return image.reshape(pair_rows, width)


def solution(mesh):
    return jax.shard_map(
        local,
        mesh=mesh,
        in_specs=(P(("gx", "gy"), None), P(("gx", "gy"), None), P(), P(), P(), P()),
        out_specs=P(("gx", "gy"), None),
        check_vma=False,
    )
```

```python
import jax
import jax.numpy as jnp
from jax import lax
from jax.experimental import pallas as pl
from jax.experimental.pallas import tpu as pltpu
from jax.sharding import PartitionSpec as P

MESH = pl.DeviceIdType.MESH
LEVELS = 8
GROUPS = 128
HALVES = GROUPS // 2
ROWS = 16
WAVES = 4
LANES = 128
HALF = LANES // 2
SPAN = 16
SCALE = 40.0
DECODE = 0.018033688011112043
DIGITS = (2, 4, 4, 4)
CODES = 2
GROUPED = (
    ((0, 0), (1, 0), (2, 0)),
    ((2, 1), (2, 2), (2, 3)),
    ((0, 1), (1, 1), (0, 2)),
    ((1, 2), (0, 3), (1, 3)),
)


def axis_of(place, stage):
    return "xyz"[(place + stage) % 3]


def odd_bits(n):
    return bin(n).count("1") % 2


def digits(d):
    return d // 64, d // 16 % 4, d // 4 % 4, d % 4


def double(a):
    twice = a[1] + a[1]
    return 1.0 - twice * a[1], twice * a[0]


def next_odd(twice, even, odd):
    return twice * even[0] - odd[0], twice * even[1] - odd[1]


def unit(half):
    sq = half * half
    sine = half * (0.999999977 + sq * (-1.66666476e-1 + sq * (8.33289965e-3 + sq * (-1.98008872e-4 + sq * 2.59046704e-6))))
    cosine = 0.99999995 + sq * (-0.49999905 + sq * (4.16635835e-2 + sq * (-1.38536951e-3 + sq * 2.3153718e-5)))
    return double((cosine, sine))


def build_matrices(real, imag, eval_real, eval_imag, mats):
    flip = lambda parity, child: (child + parity) % 2

    def halves(level):
        tr = [[real[level, c, e].astype(jnp.float32).T for e in range(2)] for c in range(2)]
        ti = [[imag[level, c, e].astype(jnp.float32).T for e in range(2)] for c in range(2)]

        def rows(kind, e, parity):
            a, b = flip(parity, 0), flip(parity, 1)
            if kind == 0:
                parts = [tr[a][e], tr[b][e], ti[a][e], ti[b][e]]
            else:
                parts = [-ti[a][e], -ti[b][e], tr[a][e], tr[b][e]]
            return jnp.concatenate(parts, 1).astype(jnp.bfloat16)

        return rows

    rows = halves(0)
    for parity in range(2):
        for e in range(2):
            for kind in range(2):
                mats[parity, (2 * e + kind) * HALF:(2 * e + kind + 1) * HALF] = rows(kind, e, parity)

    def level_body(level, _):
        rows = halves(level)
        for parity in range(2):
            for kind in range(2):
                for e in range(2):
                    at = 2 * kind + flip(parity, e)
                    mats[2 * level + parity, at * HALF:(at + 1) * HALF] = rows(kind, e, parity)
        return 0

    lax.fori_loop(1, LEVELS, level_body, 0)
    er = eval_real[...].astype(jnp.float32).T
    ei = eval_imag[...].astype(jnp.float32).T
    both = [jnp.concatenate([er, ei], 1).astype(jnp.bfloat16), jnp.concatenate([-ei, er], 1).astype(jnp.bfloat16)]
    zero = jnp.zeros((HALF, LANES), jnp.bfloat16)
    for parity in range(2):
        for kind in range(2):
            for c in range(2):
                at = 2 * kind + flip(parity, c)
                line = [both[kind], zero] if c == 0 else [zero, both[kind]]
                mats[2 * LEVELS + parity, at * HALF:(at + 1) * HALF] = jnp.concatenate(line, 1)


def tables(codes, powers):
    def body(blk, _):
        turn = lax.rem(blk + blk // 2 + blk // 4, 2)
        for s in range(2):
            for parity in range(2):
                for y in range(4):
                    k = blk * 4 + y
                    e = odd_bits(y) ^ parity ^ s
                    u = 2 * (e + turn * (1 - 2 * e)) + s
                    one = unit(jnp.log(codes(blk, y, u).astype(jnp.float32)) * DECODE)
                    twice = one[0] + one[0]
                    two = double(one)
                    three = next_odd(twice, two, one)
                    four = double(two)
                    five = next_odd(twice, four, three)
                    six = double(three)
                    all_powers = (one, two, three, four, five, six, next_odd(twice, six, five), double(four))
                    for n, value in enumerate(all_powers):
                        for i in range(2):
                            powers[n, i, s, parity, k] = value[i].astype(jnp.bfloat16)
        return 0

    lax.fori_loop(0, 8, body, 0)


def rotate(mixed, powers, level, places, re, im):
    mixed = mixed.astype(jnp.bfloat16)
    for n, at in enumerate(places):
        real = mixed[n * ROWS:(n + 1) * ROWS, :LANES]
        imag = mixed[n * ROWS:(n + 1) * ROWS, LANES:]
        cosine, sine = powers[(level, 0) + at], powers[(level, 1) + at]
        re[at] = real * cosine - imag * sine
        im[at] = real * sine + imag * cosine


def low_lanes():
    return lax.broadcasted_iota(jnp.int32, (ROWS, LANES), 1) < HALF


def flat(tiles):
    return jnp.concatenate(tiles, 0)


def combine(evens, odds, masks, mats, level, powers, re, im):
    pieces = [[[], []], [[], []]]
    for even, odd, mask in zip(evens, odds, masks):
        for kind, ref in enumerate((re, im)):
            a, b = ref[even], ref[odd]
            pieces[0][kind].append(jnp.where(mask, a, b))
            pieces[1][kind].append(jnp.where(mask, b, a))
    for parity, places in enumerate((evens, odds)):
        x = jnp.concatenate([flat(pieces[parity][0]), flat(pieces[parity][1])], 1)
        mixed = jnp.dot(x, mats[2 * level + parity], preferred_element_type=jnp.float32)
        rotate(mixed, powers, level, places, re, im)


def chain(s, weights, mats, powers, re, im):
    low = low_lanes()
    turned = jnp.logical_xor(low, jnp.broadcast_to(s == 1, low.shape))
    blocks = [range(at, at + SPAN) for at in range(0, GROUPS // 4, SPAN)]
    for ks in blocks:
        for parity in range(2):
            left, right = [], []
            for k in ks:
                bit = s if odd_bits(k) ^ parity == 0 else 1 - s
                left.append(weights(k // 4, k % 4, 2 * bit))
                right.append(weights(k // 4, k % 4, 2 * bit + 1))
            x = jnp.concatenate([flat(left), flat(right)], 1)
            mixed = jnp.dot(x, mats[parity], preferred_element_type=jnp.float32)
            rotate(mixed, powers, 0, [(s, parity, k) for k in ks], re, im)
    for level in range(1, LEVELS - 1):
        step = 1 << level - 2 if level > 1 else 0
        for ks in blocks:
            if level > 1:
                masks = [jnp.logical_not(low) if k & step else low for k in ks]
            else:
                masks = [jnp.logical_not(turned) if odd_bits(k) else turned for k in ks]
            combine([(s, 0, k) for k in ks], [(s, 1, k ^ step) for k in ks], masks, mats, level, powers, re, im)


def joint(mats, powers, re, im, put):
    low = low_lanes()
    for at in range(0, HALVES, SPAN):
        vs = range(at, at + SPAN)
        side = [odd_bits(v) for v in vs]
        evens = [(e, 0, v // 2) for e, v in zip(side, vs)]
        odds = [(1 - e, 1, v // 2) for e, v in zip(side, vs)]
        masks = [jnp.logical_not(low) if e else low for e in side]
        combine(evens, odds, masks, mats, LEVELS - 1, powers, re, im)
    for at in range(0, HALVES, SPAN):
        vs = range(at, at + SPAN)
        for parity in range(2):
            places = [(odd_bits(v) ^ parity, parity, v // 2) for v in vs]
            x = jnp.concatenate([flat([re[p] for p in places]), flat([im[p] for p in places])], 1)
            image = jnp.dot(x, mats[2 * LEVELS + parity], preferred_element_type=jnp.float32).astype(jnp.bfloat16)
            for n, v in enumerate(vs):
                for c in range(2):
                    put(c, 2 * v + places[n][0], image[n * ROWS:(n + 1) * ROWS, c * LANES:(c + 1) * LANES])


def kernel(
    weights, travel, interp_real, interp_imag, eval_real, eval_imag,
    image, last, mats, last_powers,
    held, coded, angles, reals, imags, er, ei, powers, re, im, send_sem, recv_sem, load_sem,
):
    gx, gy = lax.axis_index("gx"), lax.axis_index("gy")
    xh, z, y, u = gx // 4, gx % 4, gy // 4, gy % 4
    bits = xh + z + z // 2 + y + y // 2 + u + u // 2
    odd = bits % 2

    def peer(axis, k):
        if axis == "x":
            x = (xh * 2 + u // 2 + k // 2) % 4
            to = x % 2 * 2 + (u + k) % 2
            return (x // 2, to), (x // 2 * 4 + z, y * 4 + to)
        if axis == "y":
            p = (y + k) % 4
            return (p,), (gx, p * 4 + u)
        p = (z + k) % 4
        return (p,), (xh * 4 + p, gy)

    def part(axis, at):
        if axis == "x":
            return at[0], slice(None), slice(None), at[1]
        if axis == "y":
            return slice(None), slice(None), at[0]
        return slice(None), at[0]

    def count(axis):
        return 8 if axis == "x" else 4

    barrier = pltpu.get_barrier_semaphore()
    for axis in "xyz":
        def greet(k, _, axis=axis):
            pl.semaphore_signal(barrier, inc=1, device_id=peer(axis, k)[1], device_id_type=MESH)
            return 0
        lax.fori_loop(1, count(axis), greet, 0)
    loads = [
        pltpu.make_async_copy(travel.at[:, pl.ds(0, 8192)], angles.at[odd], load_sem.at[0]),
        pltpu.make_async_copy(travel.at[:, pl.ds(8192, 8192)], angles.at[1 - odd], load_sem.at[1]),
        pltpu.make_async_copy(interp_real, reals, load_sem.at[2]),
        pltpu.make_async_copy(interp_imag, imags, load_sem.at[3]),
        pltpu.make_async_copy(eval_real, er, load_sem.at[4]),
        pltpu.make_async_copy(eval_imag, ei, load_sem.at[5]),
    ]
    for load in loads:
        load.start()
    pl.semaphore_wait(barrier, 13)

    def go(group, stage):
        items = GROUPED[group]
        sends = {}
        for place, (stream, w) in enumerate(items):
            if stage > 0:
                land(stage - 1, stream, w)
            sends[axis_of(place, stage)] = one(stage, stream, w, axis_of(place, stage))

        def send(i, _):
            k = 2 + i - i // 2 * 3
            sends["x"][0](2 * k)
            sends["y"][0](k)
            sends["z"][0](k)
            sends["x"][0](2 * k + 1)
            return 0

        lax.fori_loop(0, 3, send, 0)
        sends["x"][0](1)
        for axis in "xyz":
            sends[axis][1]()

    def one(stage, stream, w, axis):
        if stage > 0:
            source = lambda at: held.at[(stage - 1, stream, w) + part(axis, at)]
        elif stream == CODES:
            source = lambda at: coded.at[(w,) + part(axis, at)]
        else:
            def source(at):
                index = part(axis, at)
                index = index + (slice(None),) * (4 - len(index))
                return weights.at[(stream,) + index + (pl.ds(w * ROWS, ROWS),)]
        mine = peer(axis, 0)[0]
        target = place_of(stage, stream, w).at[part(axis, mine)]

        def send(k):
            at, device = peer(axis, k)
            pltpu.make_async_remote_copy(
                src_ref=source(at), dst_ref=target,
                send_sem=send_sem.at[stage, stream, w], recv_sem=recv_sem.at[stage, stream, w],
                device_id=device, device_id_type=MESH,
            ).start()

        def keep():
            pltpu.make_async_copy(source(mine), target, recv_sem.at[stage, stream, w]).start()

        return send, keep

    def place_of(stage, stream, w):
        if isinstance(w, int) and (stage, w) == (2, WAVES - 1) and stream != CODES:
            return last.at[stream]
        return held.at[stage, stream, w]

    def land(stage, stream, w):
        place = place_of(stage, stream, w)
        pltpu.make_async_copy(place, place, recv_sem.at[stage, stream, w]).wait()

    go(2, 0)
    go(3, 0)

    loads[0].wait()
    loads[1].wait()

    def encode(hz, _):
        for low in range(8):
            at = pl.ds(pl.multiple_of((hz * 8 + low) * LANES, LANES), LANES)
            both = jnp.concatenate([angles[0, :, at], angles[1, :, at]], 0)
            code = jnp.exp2(SCALE * both).astype(jnp.bfloat16).T
            for h in range(2):
                for w in range(WAVES):
                    row = h * 64 + w * ROWS
                    coded[w, hz // 4, hz % 4, low // 2, low % 2 * 2 + h] = code[row:row + ROWS]
        return 0

    lax.fori_loop(0, 8, encode, 0)
    go(0, 0)
    go(1, 0)
    go(0, 1)
    go(1, 1)
    go(0, 2)
    for load in loads[2:]:
        load.wait()
    build_matrices(reals, imags, er, ei, mats)
    go(1, 2)
    go(2, 1)
    go(3, 1)

    def tabulate(w):
        land(2, CODES, w)
        place = last_powers if w == WAVES - 1 else powers.at[w // 2]
        tables(lambda blk, y, u: held[2, CODES, w, blk // 4, blk % 4, y, u], place)

    tabulate(0)

    def link(n, _):
        s, w = n % 2, n // 2
        land(2, s, w)
        chain(s, lambda xz, y, u: held[2, s, w, xz // 4, xz % 4, y, u], mats, powers.at[w // 2], re, im)

        @pl.when(s == 1)
        def _():
            def put(c, d, value):
                image[w, c, d] = value

            joint(mats, powers.at[w // 2], re, im, put)

        @pl.when(n == 1)
        def _():
            tabulate(1)
            go(2, 2)
            tabulate(2)
            go(3, 2)
            tabulate(3)

        return 0

    lax.fori_loop(0, 2 * (WAVES - 1), link, 0)
    land(2, 0, WAVES - 1)
    land(2, 1, WAVES - 1)

    for items in GROUPED:
        for place, (stream, w) in enumerate(items):
            for stage in range(3):
                sent = GROUPS - GROUPS // count(axis_of(place, stage))
                bytes_of = image.at[0, 0, pl.ds(0, sent)]
                pltpu.make_async_copy(bytes_of, bytes_of, send_sem.at[stage, stream, w]).wait()


def finish(done, last, mats, powers, image, re, im, staged, out_sem):
    def out(source, w):
        return pltpu.make_async_copy(source, image.at[:, :, pl.ds(w * ROWS, ROWS)], out_sem.at[w])

    for w in range(WAVES - 1):
        out(done.at[w], w).start()

    def side(s, _):
        chain(s, lambda xz, y, u: last[s, xz // 4, xz % 4, y, u], mats, powers, re, im)
        return 0

    lax.fori_loop(0, 2, side, 0)

    def put(c, d, value):
        staged[c, d] = value

    joint(mats, powers, re, im, put)
    out(staged, WAVES - 1).start()
    for w in range(WAVES - 1):
        out(done.at[w], w).wait()
    out(staged, WAVES - 1).wait()


def local(weights, travel, interp_real, interp_imag, eval_real, eval_imag):
    pair_rows, width = weights.shape
    block_rows = pair_rows // (2 * GROUPS)
    bf16, f32 = jnp.bfloat16, jnp.float32
    tiles = (2, 2, GROUPS // 4, ROWS, LANES)
    passed = pl.pallas_call(
        kernel,
        in_specs=[pl.BlockSpec(memory_space=pl.ANY)] * 6,
        out_specs=[pl.BlockSpec(memory_space=pltpu.VMEM)] * 4,
        out_shape=[
            pltpu.VMEM((WAVES - 1, 2, GROUPS, ROWS, LANES), bf16),
            pltpu.VMEM((2,) + DIGITS + (ROWS, LANES), bf16),
            pltpu.VMEM((2 * LEVELS + 2, 2 * LANES, 2 * LANES), bf16),
            pltpu.VMEM((LEVELS, 2) + tiles, bf16),
        ],
        scratch_shapes=[
            pltpu.VMEM((3, 3, WAVES) + DIGITS + (ROWS, LANES), bf16),
            pltpu.VMEM((WAVES,) + DIGITS + (ROWS, LANES), bf16),
            pltpu.VMEM((2, HALF, pair_rows // 2), f32),
            pltpu.VMEM(interp_real.shape, bf16),
            pltpu.VMEM(interp_imag.shape, bf16),
            pltpu.VMEM(eval_real.shape, bf16),
            pltpu.VMEM(eval_imag.shape, bf16),
            pltpu.VMEM((2, LEVELS, 2) + tiles, bf16),
            pltpu.VMEM(tiles, bf16),
            pltpu.VMEM(tiles, bf16),
            pltpu.SemaphoreType.DMA((3, 3, WAVES)),
            pltpu.SemaphoreType.DMA((3, 3, WAVES)),
            pltpu.SemaphoreType.DMA((6,)),
        ],
        compiler_params=pltpu.CompilerParams(
            collective_id=0, has_side_effects=True, vmem_limit_bytes=45 << 20
        ),
    )(weights.reshape((2,) + DIGITS + (block_rows, width)), travel.T, interp_real, interp_imag, eval_real, eval_imag)
    image = pl.pallas_call(
        finish,
        in_specs=[pl.BlockSpec(memory_space=pltpu.VMEM)] * 4,
        out_specs=pl.BlockSpec(memory_space=pl.ANY),
        out_shape=pltpu.HBM((2, GROUPS, block_rows, width), bf16),
        scratch_shapes=[
            pltpu.VMEM(tiles, bf16),
            pltpu.VMEM(tiles, bf16),
            pltpu.VMEM((2, GROUPS, ROWS, LANES), bf16),
            pltpu.SemaphoreType.DMA((WAVES,)),
        ],
        compiler_params=pltpu.CompilerParams(vmem_limit_bytes=8 << 20),
    )(*passed)
    return image.reshape(pair_rows, width)


def solution(mesh):
    return jax.shard_map(
        local,
        mesh=mesh,
        in_specs=(P(("gx", "gy"), None), P(("gx", "gy"), None), P(), P(), P(), P()),
        out_specs=P(("gx", "gy"), None),
        check_vma=False,
    )
```

```python
import jax
import jax.numpy as jnp
from jax import lax
from jax.experimental import pallas as pl
from jax.experimental.pallas import tpu as pltpu
from jax.sharding import PartitionSpec as P

MESH = pl.DeviceIdType.MESH
LEVELS = 8
GROUPS = 128
HALVES = GROUPS // 2
ROWS = 16
WAVES = 4
LANES = 128
HALF = LANES // 2
SPAN = 16
SCALE = 40.0
DECODE = 0.018033688011112043
DIGITS = (2, 4, 4, 4)
CODES = 2
GROUPED = (
    ((0, 0), (1, 0), (2, 0)),
    ((2, 1), (2, 2), (2, 3)),
    ((0, 1), (1, 1), (0, 2)),
    ((1, 2), (0, 3), (1, 3)),
)


def axis_of(place, stage):
    return "xyz"[(place + stage) % 3]


def odd_bits(n):
    return bin(n).count("1") % 2


def digits(d):
    return d // 64, d // 16 % 4, d // 4 % 4, d % 4


def double(a):
    twice = a[1] + a[1]
    return 1.0 - twice * a[1], twice * a[0]


def next_odd(twice, even, odd):
    return twice * even[0] - odd[0], twice * even[1] - odd[1]


def unit(half):
    sq = half * half
    sine = half * (0.999999977 + sq * (-1.66666476e-1 + sq * (8.33289965e-3 + sq * (-1.98008872e-4 + sq * 2.59046704e-6))))
    cosine = 0.99999995 + sq * (-0.49999905 + sq * (4.16635835e-2 + sq * (-1.38536951e-3 + sq * 2.3153718e-5)))
    return double((cosine, sine))


def build_matrices(real, imag, eval_real, eval_imag, mats):
    flip = lambda parity, child: (child + parity) % 2

    def halves(level):
        tr = [[real[level, c, e].astype(jnp.float32).T for e in range(2)] for c in range(2)]
        ti = [[imag[level, c, e].astype(jnp.float32).T for e in range(2)] for c in range(2)]

        def rows(kind, e, parity):
            a, b = flip(parity, 0), flip(parity, 1)
            if kind == 0:
                parts = [tr[a][e], tr[b][e], ti[a][e], ti[b][e]]
            else:
                parts = [-ti[a][e], -ti[b][e], tr[a][e], tr[b][e]]
            return jnp.concatenate(parts, 1).astype(jnp.bfloat16)

        return rows

    rows = halves(0)
    for parity in range(2):
        for e in range(2):
            for kind in range(2):
                mats[parity, (2 * e + kind) * HALF:(2 * e + kind + 1) * HALF] = rows(kind, e, parity)

    def level_body(level, _):
        rows = halves(level)
        for parity in range(2):
            for kind in range(2):
                for e in range(2):
                    at = 2 * kind + flip(parity, e)
                    mats[2 * level + parity, at * HALF:(at + 1) * HALF] = rows(kind, e, parity)
        return 0

    lax.fori_loop(1, LEVELS, level_body, 0)
    er = eval_real[...].astype(jnp.float32).T
    ei = eval_imag[...].astype(jnp.float32).T
    both = [jnp.concatenate([er, ei], 1).astype(jnp.bfloat16), jnp.concatenate([-ei, er], 1).astype(jnp.bfloat16)]
    zero = jnp.zeros((HALF, LANES), jnp.bfloat16)
    for parity in range(2):
        for kind in range(2):
            for c in range(2):
                at = 2 * kind + flip(parity, c)
                line = [both[kind], zero] if c == 0 else [zero, both[kind]]
                mats[2 * LEVELS + parity, at * HALF:(at + 1) * HALF] = jnp.concatenate(line, 1)


def tables(codes, powers):
    def body(blk, _):
        turn = lax.rem(blk + blk // 2 + blk // 4, 2)
        for s in range(2):
            for parity in range(2):
                for y in range(4):
                    k = blk * 4 + y
                    e = odd_bits(y) ^ parity ^ s
                    u = 2 * (e + turn * (1 - 2 * e)) + s
                    one = unit(jnp.log(codes(blk, y, u).astype(jnp.float32)) * DECODE)
                    twice = one[0] + one[0]
                    two = double(one)
                    three = next_odd(twice, two, one)
                    four = double(two)
                    five = next_odd(twice, four, three)
                    six = double(three)
                    all_powers = (one, two, three, four, five, six, next_odd(twice, six, five), double(four))
                    for n, value in enumerate(all_powers):
                        for i in range(2):
                            powers[n, i, s, parity, k] = value[i].astype(jnp.bfloat16)
        return 0

    lax.fori_loop(0, 8, body, 0)


def rotate(mixed, powers, level, places, re, im):
    mixed = mixed.astype(jnp.bfloat16)
    for n, at in enumerate(places):
        real = mixed[n * ROWS:(n + 1) * ROWS, :LANES]
        imag = mixed[n * ROWS:(n + 1) * ROWS, LANES:]
        cosine, sine = powers[(level, 0) + at], powers[(level, 1) + at]
        re[at] = real * cosine - imag * sine
        im[at] = real * sine + imag * cosine


def low_lanes():
    return lax.broadcasted_iota(jnp.int32, (ROWS, LANES), 1) < HALF


def flat(tiles):
    return jnp.concatenate(tiles, 0)


def combine(evens, odds, masks, mats, level, powers, re, im, source=None):
    pieces = [[[], []], [[], []]]
    for even, odd, mask in zip(evens, odds, masks):
        for kind, ref in enumerate(source or (re, im)):
            a, b = ref[even], ref[odd]
            pieces[0][kind].append(jnp.where(mask, a, b))
            pieces[1][kind].append(jnp.where(mask, b, a))
    for parity, places in enumerate((evens, odds)):
        x = jnp.concatenate([flat(pieces[parity][0]), flat(pieces[parity][1])], 1)
        mixed = jnp.dot(x, mats[2 * level + parity], preferred_element_type=jnp.float32)
        rotate(mixed, powers, level, places, re, im)


def chain(s, weights, mats, powers, re, im):
    low = low_lanes()
    turned = jnp.logical_xor(low, jnp.broadcast_to(s == 1, low.shape))
    blocks = [range(at, at + SPAN) for at in range(0, GROUPS // 4, SPAN)]
    for ks in blocks:
        for parity in range(2):
            left, right = [], []
            for k in ks:
                bit = s if odd_bits(k) ^ parity == 0 else 1 - s
                left.append(weights(k // 4, k % 4, 2 * bit))
                right.append(weights(k // 4, k % 4, 2 * bit + 1))
            x = jnp.concatenate([flat(left), flat(right)], 1)
            mixed = jnp.dot(x, mats[parity], preferred_element_type=jnp.float32)
            rotate(mixed, powers, 0, [(s, parity, k) for k in ks], re, im)
    for level in range(1, LEVELS - 1):
        step = 1 << level - 2 if level > 1 else 0
        for ks in blocks:
            if level > 1:
                masks = [jnp.logical_not(low) if k & step else low for k in ks]
            else:
                masks = [jnp.logical_not(turned) if odd_bits(k) else turned for k in ks]
            combine([(s, 0, k) for k in ks], [(s, 1, k ^ step) for k in ks], masks, mats, level, powers, re, im)


def joint(mats, powers, re, im, put, source=None):
    low = low_lanes()
    for at in range(0, HALVES, SPAN):
        vs = range(at, at + SPAN)
        side = [odd_bits(v) for v in vs]
        evens = [(e, 0, v // 2) for e, v in zip(side, vs)]
        odds = [(1 - e, 1, v // 2) for e, v in zip(side, vs)]
        masks = [jnp.logical_not(low) if e else low for e in side]
        combine(evens, odds, masks, mats, LEVELS - 1, powers, re, im, source)
    for at in range(0, HALVES, SPAN):
        vs = range(at, at + SPAN)
        for parity in range(2):
            places = [(odd_bits(v) ^ parity, parity, v // 2) for v in vs]
            x = jnp.concatenate([flat([re[p] for p in places]), flat([im[p] for p in places])], 1)
            image = jnp.dot(x, mats[2 * LEVELS + parity], preferred_element_type=jnp.float32).astype(jnp.bfloat16)
            for n, v in enumerate(vs):
                for c in range(2):
                    put(c, 2 * v + places[n][0], image[n * ROWS:(n + 1) * ROWS, c * LANES:(c + 1) * LANES])


def kernel(
    weights, travel, interp_real, interp_imag, eval_real, eval_imag,
    image, mats, re, im, eighth,
    held, coded, angles, reals, imags, er, ei, powers, send_sem, recv_sem, load_sem,
):
    gx, gy = lax.axis_index("gx"), lax.axis_index("gy")
    xh, z, y, u = gx // 4, gx % 4, gy // 4, gy % 4
    bits = xh + z + z // 2 + y + y // 2 + u + u // 2
    odd = bits % 2

    def peer(axis, k):
        if axis == "x":
            x = (xh * 2 + u // 2 + k // 2) % 4
            to = x % 2 * 2 + (u + k) % 2
            return (x // 2, to), (x // 2 * 4 + z, y * 4 + to)
        if axis == "y":
            p = (y + k) % 4
            return (p,), (gx, p * 4 + u)
        p = (z + k) % 4
        return (p,), (xh * 4 + p, gy)

    def part(axis, at):
        if axis == "x":
            return at[0], slice(None), slice(None), at[1]
        if axis == "y":
            return slice(None), slice(None), at[0]
        return slice(None), at[0]

    def count(axis):
        return 8 if axis == "x" else 4

    barrier = pltpu.get_barrier_semaphore()
    for axis in "xyz":
        def greet(k, _, axis=axis):
            pl.semaphore_signal(barrier, inc=1, device_id=peer(axis, k)[1], device_id_type=MESH)
            return 0
        lax.fori_loop(1, count(axis), greet, 0)
    loads = [
        pltpu.make_async_copy(travel.at[:, pl.ds(0, 8192)], angles.at[odd], load_sem.at[0]),
        pltpu.make_async_copy(travel.at[:, pl.ds(8192, 8192)], angles.at[1 - odd], load_sem.at[1]),
        pltpu.make_async_copy(interp_real, reals, load_sem.at[2]),
        pltpu.make_async_copy(interp_imag, imags, load_sem.at[3]),
        pltpu.make_async_copy(eval_real, er, load_sem.at[4]),
        pltpu.make_async_copy(eval_imag, ei, load_sem.at[5]),
    ]
    for load in loads:
        load.start()
    pl.semaphore_wait(barrier, 13)

    def go(group, stage):
        items = GROUPED[group]
        sends = {}
        for place, (stream, w) in enumerate(items):
            if stage > 0:
                land(stage - 1, stream, w)
            sends[axis_of(place, stage)] = one(stage, stream, w, axis_of(place, stage))

        def send(i, _):
            k = 2 + i - i // 2 * 3
            sends["x"][0](2 * k)
            sends["y"][0](k)
            sends["z"][0](k)
            sends["x"][0](2 * k + 1)
            return 0

        lax.fori_loop(0, 3, send, 0)
        sends["x"][0](1)
        for axis in "xyz":
            sends[axis][1]()

    def one(stage, stream, w, axis):
        if stage > 0:
            source = lambda at: held.at[(stage - 1, stream, w) + part(axis, at)]
        elif stream == CODES:
            source = lambda at: coded.at[(w,) + part(axis, at)]
        else:
            def source(at):
                index = part(axis, at)
                index = index + (slice(None),) * (4 - len(index))
                return weights.at[(stream,) + index + (pl.ds(w * ROWS, ROWS),)]
        mine = peer(axis, 0)[0]
        target = held.at[(stage, stream, w) + part(axis, mine)]

        def send(k):
            at, device = peer(axis, k)
            pltpu.make_async_remote_copy(
                src_ref=source(at), dst_ref=target,
                send_sem=send_sem.at[stage, stream, w], recv_sem=recv_sem.at[stage, stream, w],
                device_id=device, device_id_type=MESH,
            ).start()

        def keep():
            pltpu.make_async_copy(source(mine), target, recv_sem.at[stage, stream, w]).start()

        return send, keep

    def land(stage, stream, w):
        place = held.at[stage, stream, w]
        pltpu.make_async_copy(place, place, recv_sem.at[stage, stream, w]).wait()

    go(2, 0)
    go(3, 0)

    loads[0].wait()
    loads[1].wait()

    def encode(hz, _):
        for low in range(8):
            at = pl.ds(pl.multiple_of((hz * 8 + low) * LANES, LANES), LANES)
            both = jnp.concatenate([angles[0, :, at], angles[1, :, at]], 0)
            code = jnp.exp2(SCALE * both).astype(jnp.bfloat16).T
            for h in range(2):
                for w in range(WAVES):
                    row = h * 64 + w * ROWS
                    coded[w, hz // 4, hz % 4, low // 2, low % 2 * 2 + h] = code[row:row + ROWS]
        return 0

    lax.fori_loop(0, 8, encode, 0)
    go(0, 0)
    go(1, 0)
    go(0, 1)
    go(1, 1)
    go(0, 2)
    for load in loads[2:]:
        load.wait()
    build_matrices(reals, imags, er, ei, mats)
    go(1, 2)
    go(2, 1)
    go(3, 1)

    def slot_of(w):
        return w - (w + 2) // 3

    def sent(group, stage):
        for place, (stream, w) in enumerate(GROUPED[group]):
            blocks = GROUPS - GROUPS // count(axis_of(place, stage))
            bytes_of = image.at[0, 0, pl.ds(0, blocks)]
            pltpu.make_async_copy(bytes_of, bytes_of, send_sem.at[stage, stream, w]).wait()

    def tabulate(w):
        land(2, CODES, w)
        tables(lambda blk, y, u: held[2, CODES, w, blk // 4, blk % 4, y, u], powers.at[slot_of(w)])

    tabulate(0)

    def link(n, _):
        s, w = n % 2, n // 2
        land(2, s, w)
        chain(s, lambda xz, y, u: held[2, s, w, xz // 4, xz % 4, y, u], mats, powers.at[slot_of(w)], re, im)

        @pl.when((s == 1) & (w < WAVES - 1))
        def _():
            def put(c, d, value):
                image[w, c, d] = value

            joint(mats, powers.at[slot_of(w)], re, im, put)

        @pl.when(n == 1)
        def _():
            tabulate(1)
            go(2, 2)
            tabulate(2)
            go(3, 2)
            tabulate(3)
            for i in range(2):
                for side in range(2):
                    for parity in range(2):
                        eighth[i, side, parity] = powers[slot_of(3), LEVELS - 1, i, side, parity]
            for stage in range(2):
                for group in range(4):
                    sent(group, stage)
            sent(0, 2)
            sent(1, 2)

        return 0

    lax.fori_loop(0, 2 * WAVES, link, 0)
    sent(2, 2)
    sent(3, 2)


class Last:
    def __init__(self, ref):
        self.ref = ref

    def __getitem__(self, key):
        return self.ref[key[1:]]


def finish(done, mats, re_in, im_in, eighth, image, re, im, staged, out_sem):
    def out(source, w):
        return pltpu.make_async_copy(source, image.at[:, :, pl.ds(w * ROWS, ROWS)], out_sem.at[w])

    for w in range(WAVES - 1):
        out(done.at[w], w).start()

    def put(c, d, value):
        staged[c, d] = value

    joint(mats, Last(eighth), re, im, put, (re_in, im_in))
    out(staged, WAVES - 1).start()
    for w in range(WAVES - 1):
        out(done.at[w], w).wait()
    out(staged, WAVES - 1).wait()


def local(weights, travel, interp_real, interp_imag, eval_real, eval_imag):
    pair_rows, width = weights.shape
    block_rows = pair_rows // (2 * GROUPS)
    bf16, f32 = jnp.bfloat16, jnp.float32
    tiles = (2, 2, GROUPS // 4, ROWS, LANES)
    passed = pl.pallas_call(
        kernel,
        in_specs=[pl.BlockSpec(memory_space=pl.ANY)] * 6,
        out_specs=[pl.BlockSpec(memory_space=pltpu.VMEM)] * 5,
        out_shape=[
            pltpu.VMEM((WAVES - 1, 2, GROUPS, ROWS, LANES), bf16),
            pltpu.VMEM((2 * LEVELS + 2, 2 * LANES, 2 * LANES), bf16),
            pltpu.VMEM(tiles, bf16),
            pltpu.VMEM(tiles, bf16),
            pltpu.VMEM((2,) + tiles, bf16),
        ],
        scratch_shapes=[
            pltpu.VMEM((3, 3, WAVES) + DIGITS + (ROWS, LANES), bf16),
            pltpu.VMEM((WAVES,) + DIGITS + (ROWS, LANES), bf16),
            pltpu.VMEM((2, HALF, pair_rows // 2), f32),
            pltpu.VMEM(interp_real.shape, bf16),
            pltpu.VMEM(interp_imag.shape, bf16),
            pltpu.VMEM(eval_real.shape, bf16),
            pltpu.VMEM(eval_imag.shape, bf16),
            pltpu.VMEM((3, LEVELS, 2) + tiles, bf16),
            pltpu.SemaphoreType.DMA((3, 3, WAVES)),
            pltpu.SemaphoreType.DMA((3, 3, WAVES)),
            pltpu.SemaphoreType.DMA((6,)),
        ],
        compiler_params=pltpu.CompilerParams(
            collective_id=0, has_side_effects=True, vmem_limit_bytes=51 << 20
        ),
    )(weights.reshape((2,) + DIGITS + (block_rows, width)), travel.T, interp_real, interp_imag, eval_real, eval_imag)
    image = pl.pallas_call(
        finish,
        in_specs=[pl.BlockSpec(memory_space=pltpu.VMEM)] * 5,
        out_specs=pl.BlockSpec(memory_space=pl.ANY),
        out_shape=pltpu.HBM((2, GROUPS, block_rows, width), bf16),
        scratch_shapes=[
            pltpu.VMEM(tiles, bf16),
            pltpu.VMEM(tiles, bf16),
            pltpu.VMEM((2, GROUPS, ROWS, LANES), bf16),
            pltpu.SemaphoreType.DMA((WAVES,)),
        ],
        compiler_params=pltpu.CompilerParams(vmem_limit_bytes=8 << 20),
    )(*passed)
    return image.reshape(pair_rows, width)


def solution(mesh):
    return jax.shard_map(
        local,
        mesh=mesh,
        in_specs=(P(("gx", "gy"), None), P(("gx", "gy"), None), P(), P(), P(), P()),
        out_specs=P(("gx", "gy"), None),
        check_vma=False,
    )
```

```python
import jax
import jax.numpy as jnp
from jax import lax
from jax.experimental import pallas as pl
from jax.experimental.pallas import tpu as pltpu
from jax.sharding import PartitionSpec as P

MESH = pl.DeviceIdType.MESH
LEVELS = 8
GROUPS = 128
HALVES = GROUPS // 2
ROWS = 16
WAVES = 4
LANES = 128
HALF = LANES // 2
SPAN = 32
SCALE = 40.0
DECODE = 0.018033688011112043
DIGITS = (2, 4, 4, 4)
CODES = 2
GROUPED = (
    ((0, 0), (1, 0), (2, 0)),
    ((2, 1), (2, 2), (2, 3)),
    ((0, 1), (1, 1), (0, 2)),
    ((1, 2), (0, 3), (1, 3)),
)


def axis_of(place, stage):
    return "xyz"[(place + stage) % 3]


def odd_bits(n):
    return bin(n).count("1") % 2


def digits(d):
    return d // 64, d // 16 % 4, d // 4 % 4, d % 4


def double(a):
    twice = a[1] + a[1]
    return 1.0 - twice * a[1], twice * a[0]


def next_odd(twice, even, odd):
    return twice * even[0] - odd[0], twice * even[1] - odd[1]


def unit(half):
    sq = half * half
    sine = half * (0.999999977 + sq * (-1.66666476e-1 + sq * (8.33289965e-3 + sq * (-1.98008872e-4 + sq * 2.59046704e-6))))
    cosine = 0.99999995 + sq * (-0.49999905 + sq * (4.16635835e-2 + sq * (-1.38536951e-3 + sq * 2.3153718e-5)))
    return double((cosine, sine))


def build_matrices(real, imag, eval_real, eval_imag, mats):
    flip = lambda parity, child: (child + parity) % 2

    def halves(level):
        tr = [[real[level, c, e].astype(jnp.float32).T for e in range(2)] for c in range(2)]
        ti = [[imag[level, c, e].astype(jnp.float32).T for e in range(2)] for c in range(2)]

        def rows(kind, e, parity):
            a, b = flip(parity, 0), flip(parity, 1)
            if kind == 0:
                parts = [tr[a][e], tr[b][e], ti[a][e], ti[b][e]]
            else:
                parts = [-ti[a][e], -ti[b][e], tr[a][e], tr[b][e]]
            return jnp.concatenate(parts, 1).astype(jnp.bfloat16)

        return rows

    rows = halves(0)
    for parity in range(2):
        for e in range(2):
            for kind in range(2):
                mats[parity, (2 * e + kind) * HALF:(2 * e + kind + 1) * HALF] = rows(kind, e, parity)

    def level_body(level, _):
        rows = halves(level)
        for parity in range(2):
            for kind in range(2):
                for e in range(2):
                    at = 2 * kind + flip(parity, e)
                    mats[2 * level + parity, at * HALF:(at + 1) * HALF] = rows(kind, e, parity)
        return 0

    lax.fori_loop(1, LEVELS, level_body, 0)
    er = eval_real[...].astype(jnp.float32).T
    ei = eval_imag[...].astype(jnp.float32).T
    both = [jnp.concatenate([er, ei], 1).astype(jnp.bfloat16), jnp.concatenate([-ei, er], 1).astype(jnp.bfloat16)]
    zero = jnp.zeros((HALF, LANES), jnp.bfloat16)
    for parity in range(2):
        for kind in range(2):
            for c in range(2):
                at = 2 * kind + flip(parity, c)
                line = [both[kind], zero] if c == 0 else [zero, both[kind]]
                mats[2 * LEVELS + parity, at * HALF:(at + 1) * HALF] = jnp.concatenate(line, 1)


def tables(codes, powers):
    def body(blk, _):
        turn = lax.rem(blk + blk // 2 + blk // 4, 2)
        for s in range(2):
            for parity in range(2):
                for y in range(4):
                    k = blk * 4 + y
                    e = odd_bits(y) ^ parity ^ s
                    u = 2 * (e + turn * (1 - 2 * e)) + s
                    one = unit(jnp.log(codes(blk, y, u).astype(jnp.float32)) * DECODE)
                    twice = one[0] + one[0]
                    two = double(one)
                    three = next_odd(twice, two, one)
                    four = double(two)
                    five = next_odd(twice, four, three)
                    six = double(three)
                    all_powers = (one, two, three, four, five, six, next_odd(twice, six, five), double(four))
                    for n, value in enumerate(all_powers):
                        for i in range(2):
                            powers[n, i, s, parity, k] = value[i].astype(jnp.bfloat16)
        return 0

    lax.fori_loop(0, 8, body, 0)


def rotate(mixed, powers, level, places, re, im):
    mixed = mixed.astype(jnp.bfloat16)
    for n, at in enumerate(places):
        real = mixed[n * ROWS:(n + 1) * ROWS, :LANES]
        imag = mixed[n * ROWS:(n + 1) * ROWS, LANES:]
        cosine, sine = powers[(level, 0) + at], powers[(level, 1) + at]
        re[at] = real * cosine - imag * sine
        im[at] = real * sine + imag * cosine


def low_lanes():
    return lax.broadcasted_iota(jnp.int32, (ROWS, LANES), 1) < HALF


def flat(tiles):
    return jnp.concatenate(tiles, 0)


def combine(evens, odds, masks, mats, level, powers, re, im):
    pieces = [[[], []], [[], []]]
    for even, odd, mask in zip(evens, odds, masks):
        for kind, ref in enumerate((re, im)):
            a, b = ref[even], ref[odd]
            pieces[0][kind].append(jnp.where(mask, a, b))
            pieces[1][kind].append(jnp.where(mask, b, a))
    for parity, places in enumerate((evens, odds)):
        x = jnp.concatenate([flat(pieces[parity][0]), flat(pieces[parity][1])], 1)
        mixed = jnp.dot(x, mats[2 * level + parity], preferred_element_type=jnp.float32)
        rotate(mixed, powers, level, places, re, im)


def chain(s, weights, mats, powers, re, im):
    low = low_lanes()
    turned = jnp.logical_xor(low, jnp.broadcast_to(s == 1, low.shape))
    blocks = [range(at, at + SPAN) for at in range(0, GROUPS // 4, SPAN)]
    for ks in blocks:
        for parity in range(2):
            left, right = [], []
            for k in ks:
                bit = s if odd_bits(k) ^ parity == 0 else 1 - s
                left.append(weights(k // 4, k % 4, 2 * bit))
                right.append(weights(k // 4, k % 4, 2 * bit + 1))
            x = jnp.concatenate([flat(left), flat(right)], 1)
            mixed = jnp.dot(x, mats[parity], preferred_element_type=jnp.float32)
            rotate(mixed, powers, 0, [(s, parity, k) for k in ks], re, im)
    for level in range(1, LEVELS - 1):
        step = 1 << level - 2 if level > 1 else 0
        for ks in blocks:
            if level > 1:
                masks = [jnp.logical_not(low) if k & step else low for k in ks]
            else:
                masks = [jnp.logical_not(turned) if odd_bits(k) else turned for k in ks]
            combine([(s, 0, k) for k in ks], [(s, 1, k ^ step) for k in ks], masks, mats, level, powers, re, im)


def joint(mats, powers, re, im, put):
    low = low_lanes()
    for at in range(0, HALVES, SPAN):
        vs = range(at, at + SPAN)
        side = [odd_bits(v) for v in vs]
        evens = [(e, 0, v // 2) for e, v in zip(side, vs)]
        odds = [(1 - e, 1, v // 2) for e, v in zip(side, vs)]
        masks = [jnp.logical_not(low) if e else low for e in side]
        combine(evens, odds, masks, mats, LEVELS - 1, powers, re, im)
    for at in range(0, HALVES, SPAN):
        vs = range(at, at + SPAN)
        for parity in range(2):
            places = [(odd_bits(v) ^ parity, parity, v // 2) for v in vs]
            x = jnp.concatenate([flat([re[p] for p in places]), flat([im[p] for p in places])], 1)
            image = jnp.dot(x, mats[2 * LEVELS + parity], preferred_element_type=jnp.float32).astype(jnp.bfloat16)
            for n, v in enumerate(vs):
                for c in range(2):
                    put(c, 2 * v + places[n][0], image[n * ROWS:(n + 1) * ROWS, c * LANES:(c + 1) * LANES])


def kernel(
    weights, travel, interp_real, interp_imag, eval_real, eval_imag,
    image, last, mats, last_powers,
    held, coded, angles, reals, imags, er, ei, powers, re, im, send_sem, recv_sem, load_sem,
):
    gx, gy = lax.axis_index("gx"), lax.axis_index("gy")
    xh, z, y, u = gx // 4, gx % 4, gy // 4, gy % 4
    bits = xh + z + z // 2 + y + y // 2 + u + u // 2
    odd = bits % 2

    def peer(axis, k):
        if axis == "x":
            x = (xh * 2 + u // 2 + k // 2) % 4
            to = x % 2 * 2 + (u + k) % 2
            return (x // 2, to), (x // 2 * 4 + z, y * 4 + to)
        if axis == "y":
            p = (y + k) % 4
            return (p,), (gx, p * 4 + u)
        p = (z + k) % 4
        return (p,), (xh * 4 + p, gy)

    def part(axis, at):
        if axis == "x":
            return at[0], slice(None), slice(None), at[1]
        if axis == "y":
            return slice(None), slice(None), at[0]
        return slice(None), at[0]

    def count(axis):
        return 8 if axis == "x" else 4

    barrier = pltpu.get_barrier_semaphore()
    for axis in "xyz":
        def greet(k, _, axis=axis):
            pl.semaphore_signal(barrier, inc=1, device_id=peer(axis, k)[1], device_id_type=MESH)
            return 0
        lax.fori_loop(1, count(axis), greet, 0)
    loads = [
        pltpu.make_async_copy(travel.at[:, pl.ds(0, 8192)], angles.at[odd], load_sem.at[0]),
        pltpu.make_async_copy(travel.at[:, pl.ds(8192, 8192)], angles.at[1 - odd], load_sem.at[1]),
        pltpu.make_async_copy(interp_real, reals, load_sem.at[2]),
        pltpu.make_async_copy(interp_imag, imags, load_sem.at[3]),
        pltpu.make_async_copy(eval_real, er, load_sem.at[4]),
        pltpu.make_async_copy(eval_imag, ei, load_sem.at[5]),
    ]
    for load in loads:
        load.start()
    pl.semaphore_wait(barrier, 13)

    def go(group, stage):
        items = GROUPED[group]
        sends = {}
        for place, (stream, w) in enumerate(items):
            if stage > 0:
                land(stage - 1, stream, w)
            sends[axis_of(place, stage)] = one(stage, stream, w, axis_of(place, stage))

        def send(i, _):
            k = 2 + i - i // 2 * 3
            sends["x"][0](2 * k)
            sends["y"][0](k)
            sends["z"][0](k)
            sends["x"][0](2 * k + 1)
            return 0

        lax.fori_loop(0, 3, send, 0)
        sends["x"][0](1)
        for axis in "xyz":
            sends[axis][1]()

    def one(stage, stream, w, axis):
        if stage > 0:
            source = lambda at: held.at[(stage - 1, stream, w) + part(axis, at)]
        elif stream == CODES:
            source = lambda at: coded.at[(w,) + part(axis, at)]
        else:
            def source(at):
                index = part(axis, at)
                index = index + (slice(None),) * (4 - len(index))
                return weights.at[(stream,) + index + (pl.ds(w * ROWS, ROWS),)]
        mine = peer(axis, 0)[0]
        target = place_of(stage, stream, w).at[part(axis, mine)]

        def send(k):
            at, device = peer(axis, k)
            pltpu.make_async_remote_copy(
                src_ref=source(at), dst_ref=target,
                send_sem=send_sem.at[stage, stream, w], recv_sem=recv_sem.at[stage, stream, w],
                device_id=device, device_id_type=MESH,
            ).start()

        def keep():
            pltpu.make_async_copy(source(mine), target, recv_sem.at[stage, stream, w]).start()

        return send, keep

    def place_of(stage, stream, w):
        if isinstance(w, int) and (stage, w) == (2, WAVES - 1) and stream != CODES:
            return last.at[stream]
        return held.at[stage, stream, w]

    def land(stage, stream, w):
        place = place_of(stage, stream, w)
        pltpu.make_async_copy(place, place, recv_sem.at[stage, stream, w]).wait()

    go(2, 0)
    go(3, 0)

    loads[0].wait()
    loads[1].wait()

    def encode(hz, _):
        for low in range(8):
            at = pl.ds(pl.multiple_of((hz * 8 + low) * LANES, LANES), LANES)
            both = jnp.concatenate([angles[0, :, at], angles[1, :, at]], 0)
            code = jnp.exp2(SCALE * both).astype(jnp.bfloat16).T
            for h in range(2):
                for w in range(WAVES):
                    row = h * 64 + w * ROWS
                    coded[w, hz // 4, hz % 4, low // 2, low % 2 * 2 + h] = code[row:row + ROWS]
        return 0

    lax.fori_loop(0, 8, encode, 0)
    go(0, 0)
    go(1, 0)
    go(0, 1)
    go(1, 1)
    go(0, 2)
    for load in loads[2:]:
        load.wait()
    build_matrices(reals, imags, er, ei, mats)
    go(1, 2)
    go(2, 1)
    go(3, 1)

    def sent(group, stage):
        for place, (stream, w) in enumerate(GROUPED[group]):
            blocks = GROUPS - GROUPS // count(axis_of(place, stage))
            bytes_of = image.at[0, 0, pl.ds(0, blocks)]
            pltpu.make_async_copy(bytes_of, bytes_of, send_sem.at[stage, stream, w]).wait()

    def tabulate(w):
        land(2, CODES, w)
        place = last_powers if w == WAVES - 1 else powers.at[w // 2]
        tables(lambda blk, y, u: held[2, CODES, w, blk // 4, blk % 4, y, u], place)

    tabulate(0)

    def link(n, _):
        s, w = n % 2, n // 2
        land(2, s, w)
        chain(s, lambda xz, y, u: held[2, s, w, xz // 4, xz % 4, y, u], mats, powers.at[w // 2], re, im)

        @pl.when(s == 1)
        def _():
            def put(c, d, value):
                image[w, c, d] = value

            joint(mats, powers.at[w // 2], re, im, put)

        @pl.when(n == 1)
        def _():
            tabulate(1)
            go(2, 2)
            tabulate(2)
            go(3, 2)
            tabulate(3)
            for stage in range(2):
                for group in range(4):
                    sent(group, stage)
            sent(0, 2)
            sent(1, 2)

        return 0

    lax.fori_loop(0, 2 * (WAVES - 1), link, 0)
    land(2, 0, WAVES - 1)
    land(2, 1, WAVES - 1)
    sent(2, 2)
    sent(3, 2)


def finish(done, last, mats, powers, image, re, im, staged, out_sem):
    def out(source, w):
        return pltpu.make_async_copy(source, image.at[:, :, pl.ds(w * ROWS, ROWS)], out_sem.at[w])

    for w in range(WAVES - 1):
        out(done.at[w], w).start()

    def side(s, _):
        chain(s, lambda xz, y, u: last[s, xz // 4, xz % 4, y, u], mats, powers, re, im)
        return 0

    lax.fori_loop(0, 2, side, 0)

    def put(c, d, value):
        staged[c, d] = value

    joint(mats, powers, re, im, put)
    out(staged, WAVES - 1).start()
    for w in range(WAVES - 1):
        out(done.at[w], w).wait()
    out(staged, WAVES - 1).wait()


def local(weights, travel, interp_real, interp_imag, eval_real, eval_imag):
    pair_rows, width = weights.shape
    block_rows = pair_rows // (2 * GROUPS)
    bf16, f32 = jnp.bfloat16, jnp.float32
    tiles = (2, 2, GROUPS // 4, ROWS, LANES)
    passed = pl.pallas_call(
        kernel,
        in_specs=[pl.BlockSpec(memory_space=pl.ANY)] * 6,
        out_specs=[pl.BlockSpec(memory_space=pltpu.VMEM)] * 4,
        out_shape=[
            pltpu.VMEM((WAVES - 1, 2, GROUPS, ROWS, LANES), bf16),
            pltpu.VMEM((2,) + DIGITS + (ROWS, LANES), bf16),
            pltpu.VMEM((2 * LEVELS + 2, 2 * LANES, 2 * LANES), bf16),
            pltpu.VMEM((LEVELS, 2) + tiles, bf16),
        ],
        scratch_shapes=[
            pltpu.VMEM((3, 3, WAVES) + DIGITS + (ROWS, LANES), bf16),
            pltpu.VMEM((WAVES,) + DIGITS + (ROWS, LANES), bf16),
            pltpu.VMEM((2, HALF, pair_rows // 2), f32),
            pltpu.VMEM(interp_real.shape, bf16),
            pltpu.VMEM(interp_imag.shape, bf16),
            pltpu.VMEM(eval_real.shape, bf16),
            pltpu.VMEM(eval_imag.shape, bf16),
            pltpu.VMEM((2, LEVELS, 2) + tiles, bf16),
            pltpu.VMEM(tiles, bf16),
            pltpu.VMEM(tiles, bf16),
            pltpu.SemaphoreType.DMA((3, 3, WAVES)),
            pltpu.SemaphoreType.DMA((3, 3, WAVES)),
            pltpu.SemaphoreType.DMA((6,)),
        ],
        compiler_params=pltpu.CompilerParams(
            collective_id=0, has_side_effects=True, vmem_limit_bytes=45 << 20
        ),
    )(weights.reshape((2,) + DIGITS + (block_rows, width)), travel.T, interp_real, interp_imag, eval_real, eval_imag)
    image = pl.pallas_call(
        finish,
        in_specs=[pl.BlockSpec(memory_space=pltpu.VMEM)] * 4,
        out_specs=pl.BlockSpec(memory_space=pl.ANY),
        out_shape=pltpu.HBM((2, GROUPS, block_rows, width), bf16),
        scratch_shapes=[
            pltpu.VMEM(tiles, bf16),
            pltpu.VMEM(tiles, bf16),
            pltpu.VMEM((2, GROUPS, ROWS, LANES), bf16),
            pltpu.SemaphoreType.DMA((WAVES,)),
        ],
        compiler_params=pltpu.CompilerParams(vmem_limit_bytes=8 << 20),
    )(*passed)
    return image.reshape(pair_rows, width)


def solution(mesh):
    return jax.shard_map(
        local,
        mesh=mesh,
        in_specs=(P(("gx", "gy"), None), P(("gx", "gy"), None), P(), P(), P(), P()),
        out_specs=P(("gx", "gy"), None),
        check_vma=False,
    )
```
